32 devices in a mesh: parts: 2 (over x), xy: 16 (over z, y, core).
Axes of the slice: x: 2, y: 2, z: 4, core: 2. Of those that a mesh axis runs over, the one named last changes fastest.
Arguments:
- affinity: bfloat16 [3, 256, 64, 128], P(None, ('parts', 'xy')), parts along dimension 1, may hold values from 0 to 1
- block_scale: float32 [3, 256, 64], P(None, ('parts', 'xy')), parts along dimension 1, may hold values from 0.5 to 2
- slot_map: int32 [256, 64, 128], P(('parts', 'xy')), parts along dimension 0, may hold values from 0 to 7, as said below
- edge_list: int32 [256, 64, 8], P(('parts', 'xy')), parts along dimension 0, may hold values from 0 to 8191, as said below
- valid_count: int32 [256, 64], P(('parts', 'xy')), parts along dimension 0, may hold values from 5 to 8
- edge_home: int32 [16384], P('parts'), parts along dimension 0, may hold values from 0 to 8191, as said below
Outputs:
- edge_features: float32 [16384, 64], P(('parts', 'xy')), parts along dimension 0
The draws below stay inside these ranges and needn't reach their ends.
There are 2 independent parts, one for each index of `parts`. The reference program is written for one: setup_inputs(seed, part) draws one part's arguments, and reference() takes and returns one part's arrays. A program takes and returns all parts, laid end to end along the dimension named above; each array names one. Nothing has to cross between parts.
Inputs may be any that keep to these rules, and one draw needn't show every extreme that they name: `slot_map`: every voxel's entry is below its block's valid_count. `edge_list`: among the used entries of the blocks of one device (8 planes), at most 512 name edges whose edge_home lies in any one range [k * 512, (k + 1) * 512); in every draw some range receives exactly 512 from every device. `edge_home`: a permutation of 0 to 8191.
All inputs are finite; a program needn't handle non-finite values.
Results may differ from the reference program's by a relative error of at most 0.0003.
Values sent between devices are 32-bit elements; how exact they have to be, the bound alone decides.
A program may use at most 64 MiB of HBM per device.

```python
import math
import jax
import jax.numpy as jnp
from jax import lax

CX = 8
CY = 128
CZ = 64
SLOTS = 8
HALO = 8
FEAT = 64
E_DEV = 512
NX = 128
BPP = 64
EDGES = 8192
CAP = 512
N_XY = 16


def layout(key):
    keys = [jax.random.fold_in(key, 7000 + number) for number in range(7)]
    home = jax.random.permutation(keys[0], EDGES).astype(jnp.int32)
    inverse = jnp.argsort(home).astype(jnp.int32)
    counts = jax.random.randint(keys[1], (NX, BPP), SLOTS // 2 + 1, SLOTS + 1, dtype=jnp.int32)
    per_device = CX * BPP * SLOTS
    valid = (jnp.arange(SLOTS, dtype=jnp.int32) < counts[..., None]).reshape(N_XY, per_device)
    scores = jnp.where(valid, jax.random.randint(keys[2], (N_XY, per_device), 0, 1 << 29, dtype=jnp.int32), 1 << 30)
    order = jnp.argsort(scores, axis=1, stable=True)
    ranks = jnp.argsort(order, axis=1, stable=True).astype(jnp.int32)
    hottest = jax.random.randint(keys[3], (), 0, N_XY, dtype=jnp.int32)
    others = (ranks - CAP) % (N_XY - 1)
    others = others + (others >= hottest).astype(jnp.int32)
    target = jnp.where(ranks < CAP, hottest, others)
    within = jax.random.randint(keys[4], (N_XY, per_device), 0, E_DEV, dtype=jnp.int32)
    chosen = inverse[target * E_DEV + within]
    filler = jax.random.randint(keys[5], (N_XY, per_device), 0, EDGES, dtype=jnp.int32)
    edges = jnp.where(valid, chosen, filler).reshape(NX, BPP, SLOTS)
    slots = jax.random.randint(keys[6], (NX, BPP, 128), 0, counts[..., None], dtype=jnp.int32).reshape(NX, CZ, CY)
    return (home, edges, counts, slots)


def draw_slot_map(key, part):
    return layout(key)[3]


def draw_edge_list(key, part):
    return layout(key)[1]


def draw_valid_count(key, part):
    return layout(key)[2]


def draw_edge_home(key, part):
    return layout(key)[0]


def expand_cells(cells, along_x, along_z, along_y):
    lead, cell_x, cell_z, cell_y = cells.shape
    grown = jnp.broadcast_to(cells[:, :, None, :, None, :, None], (lead, cell_x, along_x, cell_z, along_z, cell_y, along_y))
    return grown.reshape(lead, cell_x * along_x, cell_z * along_z, cell_y * along_y)


def draw_affinity(key, part):
    keys = [jax.random.fold_in(key, 8000 + number) for number in range(4)]
    coarse_draw = jax.random.randint(keys[0], (3, NX // 8, CZ // 8, CY // 16), 0, 5, dtype=jnp.int32)
    middle_draw = jax.random.randint(keys[1], (3, NX // 2, CZ // 2, CY // 2), 0, 2, dtype=jnp.int32)
    fine_rate = jax.random.randint(keys[2], (3, NX, CZ, 1), 1, 8, dtype=jnp.int32)
    fine_draw = jax.random.randint(keys[3], (3, NX, CZ, CY), 0, 8, dtype=jnp.int32)
    fine_on = (fine_draw < fine_rate).astype(jnp.float32)
    middle_on = expand_cells((middle_draw < 1).astype(jnp.float32), 2, 2, 2)
    coarse_on = expand_cells((coarse_draw < 2).astype(jnp.float32), 8, 8, 16)
    value = 0.5 * coarse_on + 0.25 * middle_on + 0.25 * fine_on
    return value.astype(jnp.float32).astype(jnp.bfloat16)


def levels(rng, shape, split, least, high):
    level, own = 1.0, jax.random.fold_in(rng, 6)
    for dim, parts in split:
        draws = jnp.exp(jax.random.uniform(jax.random.fold_in(own, dim), (parts,), jnp.float32, least / len(split), high / len(split)))
        level = level * jnp.repeat(draws, shape[dim] // parts).reshape([-1 if axis == dim else 1 for axis in range(len(shape))])
    return level


def setup_inputs(seed: int = 0, part: int = 0) -> dict:
    splits = jax.random.split(jax.random.key(seed), 7)
    own_keys = jax.random.split(jax.random.fold_in(splits[6], part), 7)
    return {
        "affinity": draw_affinity(jax.random.fold_in(jax.random.fold_in(splits[6], part), 71), part),
        "block_scale": jnp.clip(jnp.exp(math.log(2.0) - 1.3862944 * jax.random.uniform(own_keys[1], (3, NX, BPP), jnp.float32) ** levels(own_keys[1], (3, NX, BPP), ((1, 16),), -0.2, 0.2)), 0.5, 2.0),
        "slot_map": draw_slot_map(jax.random.fold_in(jax.random.fold_in(splits[6], part), 71), part),
        "edge_list": draw_edge_list(jax.random.fold_in(jax.random.fold_in(splits[6], part), 71), part),
        "valid_count": draw_valid_count(jax.random.fold_in(jax.random.fold_in(splits[6], part), 71), part),
        "edge_home": draw_edge_home(jax.random.fold_in(jax.random.fold_in(splits[6], part), 71), part),
    }


sigma_list = (0.8, 1.3, 2.0, 3.0)


def kernel_for(sigma_value):
    offsets = jnp.arange(-HALO, HALO + 1).astype(jnp.float32)
    weights = jnp.exp(-offsets * offsets / (2.0 * sigma_value * sigma_value))
    return weights / jnp.sum(weights)


def blur_axis(field, axis, kernel):
    widths = [(0, 0)] * field.ndim
    widths[axis] = (HALO, HALO)
    padded = jnp.pad(field, widths)
    length = field.shape[axis]
    total = jnp.zeros(field.shape, jnp.float32)
    for offset in range(2 * HALO + 1):
        total = total + kernel[offset] * lax.slice_in_dim(padded, offset, offset + length, axis=axis)
    return total


def feature_rows(resp, raw):
    square = resp * resp
    pairs = []
    for scale_index in range(4):
        base = resp[3 * scale_index:3 * scale_index + 3]
        pairs += [base[0] * base[1], base[0] * base[2], base[1] * base[2]]
    ones = jnp.ones((1, resp.shape[1]), jnp.float32)
    return jnp.concatenate([resp, square, square * resp, square * square, jnp.stack(pairs), raw, ones], 0)


def finalize(table):
    count = table[:, 63]
    means = table[:, :63] / jnp.maximum(count, 1.0)[:, None]
    return jnp.concatenate([means, jnp.log1p(count)[:, None]], 1)


def reference(affinity, block_scale, slot_map, edge_list, valid_count, edge_home):
    planes = affinity.shape[1]
    dequant = (affinity.astype(jnp.float32).reshape(3, planes, BPP, 128) * block_scale[..., None]).reshape(3, planes, CZ, CY)
    fields = []
    for sigma_value in sigma_list:
        kernel = kernel_for(sigma_value)
        field = blur_axis(dequant, 1, kernel)
        field = blur_axis(field, 2, kernel)
        fields.append(blur_axis(field, 3, kernel))
    resp = jnp.concatenate(fields, 0)

    def plane_sums(inputs):
        plane_resp, plane_raw, plane_slots = inputs
        feats = feature_rows(plane_resp.reshape(12, -1), plane_raw.reshape(3, -1)).reshape(FEAT, BPP, 128)
        one_hot = (plane_slots.reshape(BPP, 128, 1) == jnp.arange(SLOTS).astype(jnp.int32)).astype(jnp.float32)
        return jnp.einsum('fbv,bvs->bsf', feats, one_hot, precision=lax.Precision.HIGHEST)

    sums = lax.map(plane_sums, (jnp.moveaxis(resp, 1, 0), jnp.moveaxis(dequant, 1, 0), slot_map))
    home = edge_home[edge_list]
    valid = jnp.arange(SLOTS).astype(jnp.int32) < valid_count[..., None]
    index = jnp.where(valid, home, EDGES).astype(jnp.int32)
    table = jnp.zeros((EDGES, FEAT), jnp.float32).at[index.reshape(-1)].add(sums.reshape(-1, FEAT), mode='drop')
    return finalize(table)
```

```python
import functools
import math
import ml_dtypes
import numpy as np
import jax
import jax.numpy as jnp
from jax import lax
from jax.experimental import pallas as pl
from jax.experimental.pallas import tpu as pltpu
from jax.sharding import PartitionSpec as P

SLOTS = 8
HALO = 8
FEAT = 64
SIGMAS = (0.8, 1.3, 2.0, 3.0)
MESH = pl.DeviceIdType.MESH
VMEM = pltpu.VMEM


def taps(sigma):
    t = np.arange(-HALO, HALO + 1).astype(np.float64)
    w = np.exp(-t * t / (2.0 * sigma * sigma))
    return (w / w.sum()).astype(np.float32)


def band(sigma, length):
    w = taps(sigma)
    rows = np.arange(length)
    shift = rows[None, :] - rows[:, None] + HALO
    inside = (shift >= 0) & (shift <= 2 * HALO)
    full = np.where(inside, w[np.clip(shift, 0, 2 * HALO)], np.float32(0)).astype(np.float32)
    high = full.astype(ml_dtypes.bfloat16)
    low = (full - high.astype(np.float32)).astype(ml_dtypes.bfloat16)
    return high, low


def split(value):
    high = value.astype(jnp.bfloat16)
    low = (value - high.astype(jnp.float32)).astype(jnp.bfloat16)
    return high, low


def bits_of(n):
    return [1 << k for k in range(n.bit_length() - 1)]


def orders(n):
    bits = bits_of(n)
    return (bits, bits[:1] + bits[2:] + bits[1:2])


def rank_of(dest, order):
    rank = jnp.zeros_like(dest)
    for bit in order:
        rank = rank * 2 + (dest // bit) % 2
    return rank


def sums_kernel(edges, banks, before, own, after, slots, along_y, along_z, elist, place, out, ext, resp, prod, rows, *tables):
    q = pl.program_id(0)
    planes, height, depth = own.shape[1:]

    @pl.when(q == 0)
    def _():
        ext[:, :HALO] = before[...]
        ext[:, HALO:HALO + planes] = own[...]
        ext[:, HALO + planes:] = after[...]
        for table in tables:
            @pl.loop(0, table.shape[0] // 64)
            def _(r):
                table[pl.ds(pl.multiple_of(r * 64, 64), 64), :] = jnp.zeros((64, 128), jnp.float32)

    weights = [taps(s) for s in SIGMAS]
    crossed = [[] for _ in SIGMAS]
    for c in range(3):
        chunks = [[] for _ in SIGMAS]
        for z in range(0, height, 16):
            mid = ext[c, q + HALO, z:z + 16, :]
            acc = [mid * float(w[HALO]) for w in weights]
            for t in range(1, HALO + 1):
                both = ext[c, q + HALO - t, z:z + 16, :] + ext[c, q + HALO + t, z:z + 16, :]
                acc = [a + both * float(w[HALO + t]) for a, w in zip(acc, weights)]
            for i in range(4):
                chunks[i].append(acc[i])
        for i in range(4):
            crossed[i].append(jnp.concatenate(chunks[i], 0))
    for i in range(4):
        high, low = split(jnp.concatenate(crossed[i], 0))
        wide = jnp.dot(jnp.concatenate([high, low], 1), along_y[i], preferred_element_type=jnp.float32)
        field = wide[:, :depth] + wide[:, depth:]
        high, low = split(field)
        highs = jnp.concatenate([high[c * height:(c + 1) * height] for c in range(3)], 1)
        lows = jnp.concatenate([low[c * height:(c + 1) * height] for c in range(3)], 1)
        stacked = jnp.concatenate([highs, lows, highs, lows], 0)
        done = jnp.dot(along_z[i], stacked, preferred_element_type=jnp.float32)
        for c in range(3):
            resp[3 * i + c] = done[:, c * depth:(c + 1) * depth]

    slot_row = lax.broadcasted_iota(jnp.int32, (SLOTS, 128), 0)
    lane_z = lax.broadcasted_iota(jnp.int32, (8, 64), 1) // SLOTS

    @pl.loop(0, height // 16)
    def _(j):
        parts = []
        for g in range(2):
            z0 = pl.multiple_of(j * 16 + g * 8, 8)
            r = [resp[k, pl.ds(z0, 8), :] for k in range(12)]
            raw = [ext[c, q + HALO, pl.ds(z0, 8), :] for c in range(3)]
            square = [a * a for a in r]
            cube = [a * b for a, b in zip(square, r)]
            fourth = [a * a for a in square]
            pairs = []
            for i in range(4):
                a, b, c = r[3 * i:3 * i + 3]
                pairs += [a * b, a * c, b * c]
            ones = [jnp.ones((8, 128), jnp.float32)]
            feats = jnp.concatenate(r + square + cube + fourth + pairs + raw + ones, 0)
            high, low = split(feats)
            lhs = jnp.concatenate([high, low], 1)
            slot = slots[0, pl.ds(z0, 8), :]
            hot = jnp.concatenate([
                (jnp.broadcast_to(slot[k:k + 1, :], (SLOTS, 128)) == slot_row).astype(jnp.float32) for k in range(8)
            ], 0).astype(jnp.bfloat16)
            rhs = jnp.concatenate([hot, hot], 1)
            prod[g] = lax.dot_general(lhs, rhs, (((1,), (1,)), ((), ())), preferred_element_type=jnp.float32)
            pieces = []
            for f in range(0, FEAT, 8):
                piece = prod[g, pl.ds(f * 8, 8, stride=8), :]
                for k in range(1, 8):
                    piece = jnp.where(lane_z == k, prod[g, pl.ds(f * 8 + k, 8, stride=8), :], piece)
                pieces.append(piece)
            parts.append(jnp.concatenate(pieces, 0))
        block = jnp.concatenate(parts, 1)
        rows[...] = jnp.transpose(jnp.concatenate([block, jnp.zeros_like(block)], 0), (1, 0))
        base = q * (height * SLOTS) + j * 128

        @pl.loop(0, 128 // 8)
        def _(k8):
            for u in range(8):
                e = k8 * 8 + u
                at = place[elist[base + e]]
                table = tables[u % banks]
                table[pl.ds(at, 1), :] += rows[pl.ds(e, 1), :]

    @pl.when(q == pl.num_programs(0) - 1)
    def _():
        tile = out.shape[2]
        low_lane = lax.broadcasted_iota(jnp.int32, (tile, 128), 1) < FEAT

        @pl.loop(0, out.shape[0] * out.shape[1])
        def _(b):
            def total(start):
                at = pl.ds(pl.multiple_of(start, 8), tile)
                value = tables[0][at, :]
                for table in tables[1:]:
                    value = value + table[at, :]
                return value
            first = total(b * 2 * tile)
            second = total(b * 2 * tile + tile)
            second = pltpu.roll(second, FEAT, 1)
            out[b // out.shape[1], b % out.shape[1]] = jnp.where(low_lane, first, second)


def reduce_kernel(n, lists, table, out, *scratch):
    count = n.bit_length() - 1
    recv = scratch[:count]
    acc = scratch[count:2 * count]
    send_sem, recv_sem = scratch[2 * count:]
    me = lax.axis_index("xy")
    part_id = lax.axis_index("parts")

    def partner(bit):
        return me + bit * (1 - 2 * ((me // bit) % 2))

    barrier = pltpu.get_barrier_semaphore()
    for bit in bits_of(n):
        pl.semaphore_signal(barrier, inc=1, device_id=(part_id, partner(bit)), device_id_type=MESH)
    pl.semaphore_wait(barrier, count)

    copies = {}

    def start(p, k):
        bit = lists[p][k]
        size = n >> (k + 1)
        mine = (me // bit) % 2
        source = table.at[p] if k == 0 else acc[k - 1].at[p]
        copy = pltpu.make_async_remote_copy(
            src_ref=source.at[pl.ds((1 - mine) * size, size)],
            dst_ref=recv[k].at[p],
            send_sem=send_sem.at[p, k],
            recv_sem=recv_sem.at[p, k],
            device_id=(part_id, partner(bit)),
            device_id_type=MESH,
        )
        copy.start()
        copies[p, k] = copy

    def finish(p, k):
        bit = lists[p][k]
        size = n >> (k + 1)
        mine = (me // bit) % 2
        source = table.at[p] if k == 0 else acc[k - 1].at[p]
        copies[p, k].wait_recv()
        if k == count - 1:
            out[p] = source[mine] + recv[k][p, 0]
        else:
            acc[k][p] = source[pl.ds(mine * size, size)] + recv[k][p]

    for p in range(2):
        start(p, 0)
    for k in range(count):
        for p in range(2):
            finish(p, k)
            if k + 1 < count:
                start(p, k + 1)
    for copy in copies.values():
        copy.wait_send()


def finalize(table):
    count = table[:, FEAT - 1:]
    means = table[:, :FEAT - 1] / jnp.maximum(count, 1.0)
    return jnp.concatenate([means, jnp.log1p(count)], 1)


def shards(affinity, block_scale, slot_map, edge_list, valid_count, edge_home):
    planes, height, depth = affinity.shape[1:]
    n = lax.axis_size("xy")
    edges = edge_home.shape[0]
    e_dev = edges // n
    tile = e_dev // 4
    lists = orders(n)
    dequant = affinity.astype(jnp.float32) * block_scale[..., None]
    up = [(i, i + 1) for i in range(n - 1)]
    down = [(j, i) for i, j in up]
    before = lax.ppermute(dequant, "xy", up)
    after = lax.ppermute(dequant, "xy", down)

    dest, inner = edge_home // e_dev, edge_home % e_dev
    half, inner = inner // (2 * tile), inner % (2 * tile)
    part, row = inner // tile, inner % tile
    rank = jnp.where(part == 0, rank_of(dest, lists[0]), rank_of(dest, lists[1]))
    place = ((part * n + rank) * 2 + half) * tile + row
    place = jnp.concatenate([place, jnp.full((128,), edges, jnp.int32)])
    valid = jnp.arange(SLOTS, dtype=jnp.int32) < valid_count[..., None]
    elist = jnp.where(valid, edge_list, edges).reshape(-1)

    ys, zs = [], []
    for sigma in SIGMAS:
        high, low = band(sigma, depth)
        ys.append(np.block([[high, low], [high, low]]))
        high, low = band(sigma, height)
        zs.append(np.concatenate([high, high, low, low], 1))
    along_y = jnp.asarray(np.stack(ys), jnp.bfloat16)
    along_z = jnp.asarray(np.stack(zs), jnp.bfloat16)
    banks = 4 if edges * 512 * 4 <= (24 << 20) else 1
    whole = pl.BlockSpec(memory_space=VMEM)
    smem = pl.BlockSpec(memory_space=pltpu.SMEM)
    table = pl.pallas_call(
        functools.partial(sums_kernel, edges, banks),
        grid=(planes,),
        out_shape=jax.ShapeDtypeStruct((2, n, tile, 128), jnp.float32),
        in_specs=[whole, whole, whole, pl.BlockSpec((1, height, depth), lambda q: (q, 0, 0)), whole, whole, smem, smem],
        out_specs=whole,
        scratch_shapes=[
            VMEM((3, planes + 2 * HALO, height, depth), jnp.float32),
            VMEM((12, height, depth), jnp.float32),
            VMEM((2, FEAT * 8, 64), jnp.float32),
            VMEM((128, 128), jnp.float32),
        ] + [VMEM((edges + 64, 128), jnp.float32)] * banks,
        compiler_params=pltpu.CompilerParams(vmem_limit_bytes=56 << 20),
    )(before, dequant, after, slot_map, along_y, along_z, elist, place)

    count = n.bit_length() - 1
    sizes = [n >> (k + 1) for k in range(count)]
    total = pl.pallas_call(
        functools.partial(reduce_kernel, n, lists),
        out_shape=jax.ShapeDtypeStruct((2, tile, 128), jnp.float32),
        in_specs=[whole],
        out_specs=whole,
        scratch_shapes=[VMEM((2, s, tile, 128), jnp.float32) for s in sizes] * 2 + [
            pltpu.SemaphoreType.DMA((2, count)),
            pltpu.SemaphoreType.DMA((2, count)),
        ],
        compiler_params=pltpu.CompilerParams(collective_id=0, has_side_effects=True, vmem_limit_bytes=56 << 20),
    )(table)
    total = total.reshape(2 * tile, 128)
    return finalize(jnp.concatenate([total[:, :FEAT], total[:, FEAT:]], 0))


def solution(mesh):
    in_specs = (
        P(None, ("parts", "xy"), None, None),
        P(None, ("parts", "xy"), None),
        P(("parts", "xy"), None, None),
        P(("parts", "xy"), None, None),
        P(("parts", "xy"), None),
        P("parts"),
    )
    out_specs = P(("parts", "xy"), None)
    return jax.shard_map(shards, mesh=mesh, in_specs=in_specs, out_specs=out_specs, check_vma=False)
```

```python
import functools
import math
import ml_dtypes
import numpy as np
import jax
import jax.numpy as jnp
from jax import lax
from jax.experimental import pallas as pl
from jax.experimental.pallas import tpu as pltpu
from jax.sharding import PartitionSpec as P

SLOTS = 8
HALO = 8
FEAT = 64
SIGMAS = (0.8, 1.3, 2.0, 3.0)
MESH = pl.DeviceIdType.MESH
VMEM = pltpu.VMEM


def taps(sigma):
    t = np.arange(-HALO, HALO + 1).astype(np.float64)
    w = np.exp(-t * t / (2.0 * sigma * sigma))
    return (w / w.sum()).astype(np.float32)


def band(sigma, length):
    w = taps(sigma)
    rows = np.arange(length)
    shift = rows[None, :] - rows[:, None] + HALO
    inside = (shift >= 0) & (shift <= 2 * HALO)
    full = np.where(inside, w[np.clip(shift, 0, 2 * HALO)], np.float32(0)).astype(np.float32)
    high = full.astype(ml_dtypes.bfloat16)
    low = (full - high.astype(np.float32)).astype(ml_dtypes.bfloat16)
    return high, low


def split(value):
    high = value.astype(jnp.bfloat16)
    low = (value - high.astype(jnp.float32)).astype(jnp.bfloat16)
    return high, low


def bits_of(n):
    return [1 << k for k in range(n.bit_length() - 1)]


def orders(n):
    bits = bits_of(n)
    late = bits[:1] + bits[2:] + bits[1:2]
    return (bits, late, bits, bits)


def rank_of(dest, order):
    rank = jnp.zeros_like(dest)
    for bit in order:
        rank = rank * 2 + (dest // bit) % 2
    return rank


def sums_kernel(edges, banks, before, own, after, slots, along_y, along_z, elist, place, out, ext, resp, prod, rows, *tables):
    q = pl.program_id(0)
    planes, height, depth = own.shape[1:]

    def add_rows(base):
        for e in range(128):
            at = place[elist[base + e]]
            table = tables[e % banks]
            table[pl.ds(at, 1), :] += rows[e:e + 1, :]

    @pl.when(q == 0)
    def _():
        rows[...] = jnp.zeros_like(rows)
        ext[:, :HALO] = before[...]
        ext[:, HALO:HALO + planes] = own[...]
        ext[:, HALO + planes:] = after[...]
        for table in tables:
            @pl.loop(0, table.shape[0] // 64)
            def _(r):
                table[pl.ds(pl.multiple_of(r * 64, 64), 64), :] = jnp.zeros((64, 128), jnp.float32)

    weights = [taps(s) for s in SIGMAS]
    crossed = [[] for _ in SIGMAS]
    for c in range(3):
        chunks = [[] for _ in SIGMAS]
        for z in range(0, height, 16):
            mid = ext[c, q + HALO, z:z + 16, :]
            acc = [mid * float(w[HALO]) for w in weights]
            for t in range(1, HALO + 1):
                both = ext[c, q + HALO - t, z:z + 16, :] + ext[c, q + HALO + t, z:z + 16, :]
                acc = [a + both * float(w[HALO + t]) for a, w in zip(acc, weights)]
            for i in range(4):
                chunks[i].append(acc[i])
        for i in range(4):
            crossed[i].append(jnp.concatenate(chunks[i], 0))
    for i in range(4):
        high, low = split(jnp.concatenate(crossed[i], 0))
        wide = jnp.dot(jnp.concatenate([high, low], 1), along_y[i], preferred_element_type=jnp.float32)
        field = wide[:, :depth] + wide[:, depth:]
        high, low = split(field)
        highs = jnp.concatenate([high[c * height:(c + 1) * height] for c in range(3)], 1)
        lows = jnp.concatenate([low[c * height:(c + 1) * height] for c in range(3)], 1)
        stacked = jnp.concatenate([highs, lows, highs, lows], 0)
        done = jnp.dot(along_z[i], stacked, preferred_element_type=jnp.float32)
        for c in range(3):
            resp[3 * i + c] = done[:, c * depth:(c + 1) * depth]

    slot_row = lax.broadcasted_iota(jnp.int32, (SLOTS, 128), 0)
    lane_z = lax.broadcasted_iota(jnp.int32, (8, 64), 1) // SLOTS

    @pl.loop(0, height // 16)
    def _(j):
        add_rows(jnp.maximum(q * (height * SLOTS) + j * 128 - 128, 0))
        parts = []
        for g in range(2):
            z0 = pl.multiple_of(j * 16 + g * 8, 8)
            r = [resp[k, pl.ds(z0, 8), :] for k in range(12)]
            raw = [ext[c, q + HALO, pl.ds(z0, 8), :] for c in range(3)]
            square = [a * a for a in r]
            cube = [a * b for a, b in zip(square, r)]
            fourth = [a * a for a in square]
            pairs = []
            for i in range(4):
                a, b, c = r[3 * i:3 * i + 3]
                pairs += [a * b, a * c, b * c]
            ones = [jnp.ones((8, 128), jnp.float32)]
            feats = jnp.concatenate(r + square + cube + fourth + pairs + raw + ones, 0)
            high, low = split(feats)
            lhs = jnp.concatenate([high, low], 1)
            slot = slots[0, pl.ds(z0, 8), :]
            hot = jnp.concatenate([
                (jnp.broadcast_to(slot[k:k + 1, :], (SLOTS, 128)) == slot_row).astype(jnp.float32) for k in range(8)
            ], 0).astype(jnp.bfloat16)
            rhs = jnp.concatenate([hot, hot], 1)
            prod[g] = lax.dot_general(lhs, rhs, (((1,), (1,)), ((), ())), preferred_element_type=jnp.float32)
            pieces = []
            for f in range(0, FEAT, 8):
                piece = prod[g, pl.ds(f * 8, 8, stride=8), :]
                for k in range(1, 8):
                    piece = jnp.where(lane_z == k, prod[g, pl.ds(f * 8 + k, 8, stride=8), :], piece)
                pieces.append(piece)
            parts.append(jnp.concatenate(pieces, 0))
        block = jnp.concatenate(parts, 1)
        rows[...] = jnp.transpose(jnp.concatenate([block, jnp.zeros_like(block)], 0), (1, 0))

    @pl.when(q == pl.num_programs(0) - 1)
    def _():
        add_rows(planes * height * SLOTS - 128)
        tile = out.shape[2]
        low_lane = lax.broadcasted_iota(jnp.int32, (tile, 128), 1) < FEAT

        @pl.loop(0, out.shape[0] * out.shape[1])
        def _(b):
            def total(start):
                at = pl.ds(pl.multiple_of(start, 8), tile)
                value = tables[0][at, :]
                for table in tables[1:]:
                    value = value + table[at, :]
                return value
            first = total(b * 2 * tile)
            second = total(b * 2 * tile + tile)
            second = pltpu.roll(second, FEAT, 1)
            out[b // out.shape[1], b % out.shape[1]] = jnp.where(low_lane, first, second)


def reduce_kernel(n, lists, table, out, *scratch):
    count = n.bit_length() - 1
    recv = scratch[:count]
    acc = scratch[count:2 * count]
    send_sem, recv_sem = scratch[2 * count:]
    me = lax.axis_index("xy")
    part_id = lax.axis_index("parts")

    def partner(bit):
        return me + bit * (1 - 2 * ((me // bit) % 2))

    barrier = pltpu.get_barrier_semaphore()
    for bit in bits_of(n):
        pl.semaphore_signal(barrier, inc=1, device_id=(part_id, partner(bit)), device_id_type=MESH)
    pl.semaphore_wait(barrier, count)

    copies = {}

    def start(p, k):
        bit = lists[p][k]
        size = n >> (k + 1)
        mine = (me // bit) % 2
        source = table.at[p] if k == 0 else acc[k - 1].at[p]
        copy = pltpu.make_async_remote_copy(
            src_ref=source.at[pl.ds((1 - mine) * size, size)],
            dst_ref=recv[k].at[p],
            send_sem=send_sem.at[p, k],
            recv_sem=recv_sem.at[p, k],
            device_id=(part_id, partner(bit)),
            device_id_type=MESH,
        )
        copy.start()
        copies[p, k] = copy

    def finish(p, k):
        bit = lists[p][k]
        size = n >> (k + 1)
        mine = (me // bit) % 2
        source = table.at[p] if k == 0 else acc[k - 1].at[p]
        copies[p, k].wait_recv()
        if k == count - 1:
            out[p] = source[mine] + recv[k][p, 0]
        else:
            acc[k][p] = source[pl.ds(mine * size, size)] + recv[k][p]

    for p in range(len(lists)):
        start(p, 0)
    for k in range(count):
        for p in range(len(lists)):
            finish(p, k)
            if k + 1 < count:
                start(p, k + 1)
    for copy in copies.values():
        copy.wait_send()


def finalize(table):
    count = table[:, FEAT - 1:]
    means = table[:, :FEAT - 1] / jnp.maximum(count, 1.0)
    return jnp.concatenate([means, jnp.log1p(count)], 1)


def shards(affinity, block_scale, slot_map, edge_list, valid_count, edge_home):
    planes, height, depth = affinity.shape[1:]
    n = lax.axis_size("xy")
    edges = edge_home.shape[0]
    e_dev = edges // n
    lists = orders(n)
    parts = len(lists)
    tile = e_dev // (2 * parts)
    dequant = affinity.astype(jnp.float32) * block_scale[..., None]
    up = [(i, i + 1) for i in range(n - 1)]
    down = [(j, i) for i, j in up]
    before = lax.ppermute(dequant, "xy", up)
    after = lax.ppermute(dequant, "xy", down)

    dest, inner = edge_home // e_dev, edge_home % e_dev
    half, inner = inner // (parts * tile), inner % (parts * tile)
    part, row = inner // tile, inner % tile
    rank = jnp.where(part == 1, rank_of(dest, lists[1]), rank_of(dest, lists[0]))
    place = ((part * n + rank) * 2 + half) * tile + row
    place = jnp.concatenate([place, jnp.full((128,), edges, jnp.int32)])
    valid = jnp.arange(SLOTS, dtype=jnp.int32) < valid_count[..., None]
    elist = jnp.where(valid, edge_list, edges).reshape(-1)

    ys, zs = [], []
    for sigma in SIGMAS:
        high, low = band(sigma, depth)
        ys.append(np.block([[high, low], [high, low]]))
        high, low = band(sigma, height)
        zs.append(np.concatenate([high, high, low, low], 1))
    along_y = jnp.asarray(np.stack(ys), jnp.bfloat16)
    along_z = jnp.asarray(np.stack(zs), jnp.bfloat16)
    banks = 4 if edges * 512 * 4 <= (24 << 20) else 1
    whole = pl.BlockSpec(memory_space=VMEM)
    smem = pl.BlockSpec(memory_space=pltpu.SMEM)
    table = pl.pallas_call(
        functools.partial(sums_kernel, edges, banks),
        grid=(planes,),
        out_shape=jax.ShapeDtypeStruct((parts, n, tile, 128), jnp.float32),
        in_specs=[whole, whole, whole, pl.BlockSpec((1, height, depth), lambda q: (q, 0, 0)), whole, whole, smem, smem],
        out_specs=whole,
        scratch_shapes=[
            VMEM((3, planes + 2 * HALO, height, depth), jnp.float32),
            VMEM((12, height, depth), jnp.float32),
            VMEM((2, FEAT * 8, 64), jnp.float32),
            VMEM((128, 128), jnp.float32),
        ] + [VMEM((edges + 64, 128), jnp.float32)] * banks,
        compiler_params=pltpu.CompilerParams(vmem_limit_bytes=56 << 20),
    )(before, dequant, after, slot_map, along_y, along_z, elist, place)

    count = n.bit_length() - 1
    sizes = [n >> (k + 1) for k in range(count)]
    total = pl.pallas_call(
        functools.partial(reduce_kernel, n, lists),
        out_shape=jax.ShapeDtypeStruct((parts, tile, 128), jnp.float32),
        in_specs=[whole],
        out_specs=whole,
        scratch_shapes=[VMEM((parts, s, tile, 128), jnp.float32) for s in sizes] * 2 + [
            pltpu.SemaphoreType.DMA((parts, count)),
            pltpu.SemaphoreType.DMA((parts, count)),
        ],
        compiler_params=pltpu.CompilerParams(collective_id=0, has_side_effects=True, vmem_limit_bytes=56 << 20),
    )(table)
    total = total.reshape(parts * tile, 128)
    return finalize(jnp.concatenate([total[:, :FEAT], total[:, FEAT:]], 0))


def solution(mesh):
    in_specs = (
        P(None, ("parts", "xy"), None, None),
        P(None, ("parts", "xy"), None),
        P(("parts", "xy"), None, None),
        P(("parts", "xy"), None, None),
        P(("parts", "xy"), None),
        P("parts"),
    )
    out_specs = P(("parts", "xy"), None)
    return jax.shard_map(shards, mesh=mesh, in_specs=in_specs, out_specs=out_specs, check_vma=False)
```

```python
import functools
import math
import ml_dtypes
import numpy as np
import jax
import jax.numpy as jnp
from jax import lax
from jax.experimental import pallas as pl
from jax.experimental.pallas import tpu as pltpu
from jax.sharding import PartitionSpec as P

SLOTS = 8
HALO = 8
FEAT = 64
SIGMAS = (0.8, 1.3, 2.0, 3.0)
MESH = pl.DeviceIdType.MESH
VMEM = pltpu.VMEM


def taps(sigma):
    t = np.arange(-HALO, HALO + 1).astype(np.float64)
    w = np.exp(-t * t / (2.0 * sigma * sigma))
    return (w / w.sum()).astype(np.float32)


def band(sigma, length):
    w = taps(sigma)
    rows = np.arange(length)
    shift = rows[None, :] - rows[:, None] + HALO
    inside = (shift >= 0) & (shift <= 2 * HALO)
    full = np.where(inside, w[np.clip(shift, 0, 2 * HALO)], np.float32(0)).astype(np.float32)
    high = full.astype(ml_dtypes.bfloat16)
    low = (full - high.astype(np.float32)).astype(ml_dtypes.bfloat16)
    return high, low


def split(value):
    high = value.astype(jnp.bfloat16)
    low = (value - high.astype(jnp.float32)).astype(jnp.bfloat16)
    return high, low


def bits_of(n):
    return [1 << k for k in range(n.bit_length() - 1)]


def orders(n):
    bits = bits_of(n)
    late = bits[:1] + bits[2:] + bits[1:2]
    return (bits, late, bits, bits)


def rank_of(dest, order):
    rank = jnp.zeros_like(dest)
    for bit in order:
        rank = rank * 2 + (dest // bit) % 2
    return rank


def blur_kernel(own, along_y, along_z, out, ext, send_sem, recv_sem):
    planes, height, depth = own.shape[1:]
    n = lax.axis_size("xy")
    me = lax.axis_index("xy")
    part_id = lax.axis_index("parts")
    has_left, has_right = me > 0, me < n - 1
    left, right = (part_id, me - 1), (part_id, me + 1)
    barrier = pltpu.get_barrier_semaphore()

    for there, device in ((has_left, left), (has_right, right)):
        @pl.when(there)
        def _():
            pl.semaphore_signal(barrier, inc=1, device_id=device, device_id_type=MESH)
    inside = jnp.logical_and(has_left, has_right)

    @pl.when(inside)
    def _():
        pl.semaphore_wait(barrier, 2)

    @pl.when(jnp.logical_and(jnp.logical_not(inside), n > 1))
    def _():
        pl.semaphore_wait(barrier, 1)

    def to_right(p):
        return pltpu.make_async_remote_copy(
            src_ref=own.at[:, p], dst_ref=ext.at[:, p],
            send_sem=send_sem.at[0, p], recv_sem=recv_sem.at[0, p],
            device_id=right, device_id_type=MESH)

    def to_left(p):
        return pltpu.make_async_remote_copy(
            src_ref=own.at[:, p], dst_ref=ext.at[:, HALO + planes + p],
            send_sem=send_sem.at[1, p], recv_sem=recv_sem.at[1, p],
            device_id=left, device_id_type=MESH)

    @pl.when(has_right)
    def _():
        for p in reversed(range(planes)):
            to_right(p).start()

    @pl.when(has_left)
    def _():
        for p in range(planes):
            to_left(p).start()

    ext[:, HALO:HALO + planes] = own[...]

    @pl.when(jnp.logical_not(has_left))
    def _():
        ext[:, :HALO] = jnp.zeros((3, HALO, height, depth), jnp.float32)

    @pl.when(jnp.logical_not(has_right))
    def _():
        ext[:, HALO + planes:] = jnp.zeros((3, HALO, height, depth), jnp.float32)

    def need(low, high):
        @pl.when(has_left)
        def _():
            to_right(low).wait_recv()

        @pl.when(has_right)
        def _():
            to_left(high).wait_recv()

    middle = planes // 2
    for p in range(middle):
        need(planes - 1 - p, p)

    weights = [taps(s) for s in SIGMAS]

    @pl.loop(0, middle)
    def _(step):
        need(middle - 1 - step, middle + step)
        for q in (middle - 1 - step, middle + step):
            crossed = [[] for _ in SIGMAS]
            for c in range(3):
                chunks = [[] for _ in SIGMAS]
                for z in range(0, height, 16):
                    mid = ext[c, q + HALO, z:z + 16, :]
                    acc = [mid * float(w[HALO]) for w in weights]
                    for t in range(1, HALO + 1):
                        both = ext[c, q + HALO - t, z:z + 16, :] + ext[c, q + HALO + t, z:z + 16, :]
                        acc = [a + both * float(w[HALO + t]) for a, w in zip(acc, weights)]
                    for i in range(4):
                        chunks[i].append(acc[i])
                for i in range(4):
                    crossed[i].append(jnp.concatenate(chunks[i], 0))
            for i in range(4):
                high, low = split(jnp.concatenate(crossed[i], 0))
                wide = jnp.dot(jnp.concatenate([high, low], 1), along_y[i], preferred_element_type=jnp.float32)
                field = wide[:, :depth] + wide[:, depth:]
                high, low = split(field)
                highs = jnp.concatenate([high[c * height:(c + 1) * height] for c in range(3)], 1)
                lows = jnp.concatenate([low[c * height:(c + 1) * height] for c in range(3)], 1)
                stacked = jnp.concatenate([highs, lows, highs, lows], 0)
                done = jnp.dot(along_z[i], stacked, preferred_element_type=jnp.float32)
                for c in range(3):
                    out[q, 3 * i + c] = done[:, c * depth:(c + 1) * depth]

    @pl.when(has_right)
    def _():
        for p in range(planes):
            to_right(p).wait_send()

    @pl.when(has_left)
    def _():
        for p in range(planes):
            to_left(p).wait_send()


def sums_kernel(planes, banks, own, resp, slots, elist, place, out, prod, rows, *tables):
    q = pl.program_id(0)
    height = own.shape[2]

    def add_rows(base):
        for e in range(128):
            at = place[elist[base + e]]
            table = tables[e % banks]
            table[pl.ds(at, 1), :] += rows[e:e + 1, :]

    @pl.when(q == 0)
    def _():
        rows[...] = jnp.zeros_like(rows)
        for table in tables:
            @pl.loop(0, table.shape[0] // 64)
            def _(r):
                table[pl.ds(pl.multiple_of(r * 64, 64), 64), :] = jnp.zeros((64, 128), jnp.float32)

    slot_row = lax.broadcasted_iota(jnp.int32, (SLOTS, 128), 0)
    lane_z = lax.broadcasted_iota(jnp.int32, (8, 64), 1) // SLOTS

    @pl.loop(0, height // 16)
    def _(j):
        add_rows(jnp.maximum(q * (height * SLOTS) + j * 128 - 128, 0))
        parts = []
        for g in range(2):
            z0 = pl.multiple_of(j * 16 + g * 8, 8)
            r = [resp[0, k, pl.ds(z0, 8), :] for k in range(12)]
            raw = [own[c, 0, pl.ds(z0, 8), :] for c in range(3)]
            square = [a * a for a in r]
            cube = [a * b for a, b in zip(square, r)]
            fourth = [a * a for a in square]
            pairs = []
            for i in range(4):
                a, b, c = r[3 * i:3 * i + 3]
                pairs += [a * b, a * c, b * c]
            ones = [jnp.ones((8, 128), jnp.float32)]
            feats = jnp.concatenate(r + square + cube + fourth + pairs + raw + ones, 0)
            high, low = split(feats)
            lhs = jnp.concatenate([high, low], 1)
            slot = slots[0, pl.ds(z0, 8), :]
            hot = jnp.concatenate([
                (jnp.broadcast_to(slot[k:k + 1, :], (SLOTS, 128)) == slot_row).astype(jnp.float32) for k in range(8)
            ], 0).astype(jnp.bfloat16)
            rhs = jnp.concatenate([hot, hot], 1)
            prod[g] = lax.dot_general(lhs, rhs, (((1,), (1,)), ((), ())), preferred_element_type=jnp.float32)
            pieces = []
            for f in range(0, FEAT, 8):
                piece = prod[g, pl.ds(f * 8, 8, stride=8), :]
                for k in range(1, 8):
                    piece = jnp.where(lane_z == k, prod[g, pl.ds(f * 8 + k, 8, stride=8), :], piece)
                pieces.append(piece)
            parts.append(jnp.concatenate(pieces, 0))
        block = jnp.concatenate(parts, 1)
        rows[...] = jnp.transpose(jnp.concatenate([block, jnp.zeros_like(block)], 0), (1, 0))

    @pl.when(q == pl.num_programs(0) - 1)
    def _():
        add_rows(planes * height * SLOTS - 128)
        tile = out.shape[2]
        low_lane = lax.broadcasted_iota(jnp.int32, (tile, 128), 1) < FEAT

        @pl.loop(0, out.shape[0] * out.shape[1])
        def _(b):
            def total(start):
                at = pl.ds(pl.multiple_of(start, 8), tile)
                value = tables[0][at, :]
                for table in tables[1:]:
                    value = value + table[at, :]
                return value
            first = total(b * 2 * tile)
            second = total(b * 2 * tile + tile)
            second = pltpu.roll(second, FEAT, 1)
            out[b // out.shape[1], b % out.shape[1]] = jnp.where(low_lane, first, second)


def reduce_kernel(n, lists, table, out, *scratch):
    count = n.bit_length() - 1
    recv = scratch[:count]
    acc = scratch[count:2 * count]
    send_sem, recv_sem = scratch[2 * count:]
    me = lax.axis_index("xy")
    part_id = lax.axis_index("parts")

    def partner(bit):
        return me + bit * (1 - 2 * ((me // bit) % 2))

    barrier = pltpu.get_barrier_semaphore()
    for bit in bits_of(n):
        pl.semaphore_signal(barrier, inc=1, device_id=(part_id, partner(bit)), device_id_type=MESH)
    pl.semaphore_wait(barrier, count)

    copies = {}

    def start(p, k):
        bit = lists[p][k]
        size = n >> (k + 1)
        mine = (me // bit) % 2
        source = table.at[p] if k == 0 else acc[k - 1].at[p]
        copy = pltpu.make_async_remote_copy(
            src_ref=source.at[pl.ds((1 - mine) * size, size)],
            dst_ref=recv[k].at[p],
            send_sem=send_sem.at[p, k],
            recv_sem=recv_sem.at[p, k],
            device_id=(part_id, partner(bit)),
            device_id_type=MESH,
        )
        copy.start()
        copies[p, k] = copy

    def finish(p, k):
        bit = lists[p][k]
        size = n >> (k + 1)
        mine = (me // bit) % 2
        source = table.at[p] if k == 0 else acc[k - 1].at[p]
        copies[p, k].wait_recv()
        if k == count - 1:
            out[p] = source[mine] + recv[k][p, 0]
        else:
            acc[k][p] = source[pl.ds(mine * size, size)] + recv[k][p]

    for p in range(len(lists)):
        start(p, 0)
    for k in range(count):
        for p in range(len(lists)):
            finish(p, k)
            if k + 1 < count:
                start(p, k + 1)
    for copy in copies.values():
        copy.wait_send()


def finalize(table):
    count = table[:, FEAT - 1:]
    means = table[:, :FEAT - 1] / jnp.maximum(count, 1.0)
    return jnp.concatenate([means, jnp.log1p(count)], 1)


def shards(affinity, block_scale, slot_map, edge_list, valid_count, edge_home):
    planes, height, depth = affinity.shape[1:]
    n = lax.axis_size("xy")
    edges = edge_home.shape[0]
    e_dev = edges // n
    lists = orders(n)
    parts = len(lists)
    tile = e_dev // (2 * parts)
    dequant = affinity.astype(jnp.float32) * block_scale[..., None]

    dest, inner = edge_home // e_dev, edge_home % e_dev
    half, inner = inner // (parts * tile), inner % (parts * tile)
    part, row = inner // tile, inner % tile
    rank = jnp.where(part == 1, rank_of(dest, lists[1]), rank_of(dest, lists[0]))
    place = ((part * n + rank) * 2 + half) * tile + row
    place = jnp.concatenate([place, jnp.full((128,), edges, jnp.int32)])
    valid = jnp.arange(SLOTS, dtype=jnp.int32) < valid_count[..., None]
    elist = jnp.where(valid, edge_list, edges).reshape(-1)

    ys, zs = [], []
    for sigma in SIGMAS:
        high, low = band(sigma, depth)
        ys.append(np.block([[high, low], [high, low]]))
        high, low = band(sigma, height)
        zs.append(np.concatenate([high, high, low, low], 1))
    along_y = jnp.asarray(np.stack(ys), jnp.bfloat16)
    along_z = jnp.asarray(np.stack(zs), jnp.bfloat16)
    banks = 4 if edges * 512 * 4 <= (24 << 20) else 1
    whole = pl.BlockSpec(memory_space=VMEM)
    smem = pl.BlockSpec(memory_space=pltpu.SMEM)
    resp = pl.pallas_call(
        blur_kernel,
        out_shape=jax.ShapeDtypeStruct((planes, 12, height, depth), jnp.float32),
        in_specs=[whole, whole, whole],
        out_specs=whole,
        scratch_shapes=[
            VMEM((3, planes + 2 * HALO, height, depth), jnp.float32),
            pltpu.SemaphoreType.DMA((2, planes)),
            pltpu.SemaphoreType.DMA((2, planes)),
        ],
        compiler_params=pltpu.CompilerParams(collective_id=1, has_side_effects=True, vmem_limit_bytes=56 << 20),
    )(dequant, along_y, along_z)
    table = pl.pallas_call(
        functools.partial(sums_kernel, planes, banks),
        grid=(planes,),
        out_shape=jax.ShapeDtypeStruct((parts, n, tile, 128), jnp.float32),
        in_specs=[
            pl.BlockSpec((3, 1, height, depth), lambda q: (0, q, 0, 0)),
            pl.BlockSpec((1, 12, height, depth), lambda q: (q, 0, 0, 0)),
            pl.BlockSpec((1, height, depth), lambda q: (q, 0, 0)),
            smem, smem,
        ],
        out_specs=whole,
        scratch_shapes=[
            VMEM((2, FEAT * 8, 64), jnp.float32),
            VMEM((128, 128), jnp.float32),
        ] + [VMEM((edges + 64, 128), jnp.float32)] * banks,
        compiler_params=pltpu.CompilerParams(vmem_limit_bytes=56 << 20),
    )(dequant, resp, slot_map, elist, place)

    count = n.bit_length() - 1
    sizes = [n >> (k + 1) for k in range(count)]
    total = pl.pallas_call(
        functools.partial(reduce_kernel, n, lists),
        out_shape=jax.ShapeDtypeStruct((parts, tile, 128), jnp.float32),
        in_specs=[whole],
        out_specs=whole,
        scratch_shapes=[VMEM((parts, s, tile, 128), jnp.float32) for s in sizes] * 2 + [
            pltpu.SemaphoreType.DMA((parts, count)),
            pltpu.SemaphoreType.DMA((parts, count)),
        ],
        compiler_params=pltpu.CompilerParams(collective_id=0, has_side_effects=True, vmem_limit_bytes=56 << 20),
    )(table)
    total = total.reshape(parts * tile, 128)
    return finalize(jnp.concatenate([total[:, :FEAT], total[:, FEAT:]], 0))


def solution(mesh):
    in_specs = (
        P(None, ("parts", "xy"), None, None),
        P(None, ("parts", "xy"), None),
        P(("parts", "xy"), None, None),
        P(("parts", "xy"), None, None),
        P(("parts", "xy"), None),
        P("parts"),
    )
    out_specs = P(("parts", "xy"), None)
    return jax.shard_map(shards, mesh=mesh, in_specs=in_specs, out_specs=out_specs, check_vma=False)
```

```python
import functools
import math
import ml_dtypes
import numpy as np
import jax
import jax.numpy as jnp
from jax import lax
from jax.experimental import pallas as pl
from jax.experimental.pallas import tpu as pltpu
from jax.sharding import PartitionSpec as P

SLOTS = 8
HALO = 8
FEAT = 64
SIGMAS = (0.8, 1.3, 2.0, 3.0)
MESH = pl.DeviceIdType.MESH
VMEM = pltpu.VMEM


def taps(sigma):
    t = np.arange(-HALO, HALO + 1).astype(np.float64)
    w = np.exp(-t * t / (2.0 * sigma * sigma))
    return (w / w.sum()).astype(np.float32)


def band(sigma, length):
    w = taps(sigma)
    rows = np.arange(length)
    shift = rows[None, :] - rows[:, None] + HALO
    inside = (shift >= 0) & (shift <= 2 * HALO)
    full = np.where(inside, w[np.clip(shift, 0, 2 * HALO)], np.float32(0)).astype(np.float32)
    high = full.astype(ml_dtypes.bfloat16)
    low = (full - high.astype(np.float32)).astype(ml_dtypes.bfloat16)
    return high, low


def split(value):
    high = value.astype(jnp.bfloat16)
    low = (value - high.astype(jnp.float32)).astype(jnp.bfloat16)
    return high, low


def bits_of(n):
    return [1 << k for k in range(n.bit_length() - 1)]


def orders(n):
    bits = bits_of(n)
    late = bits[:1] + bits[2:] + bits[1:2]
    return (bits, late, bits, bits)


def rank_of(dest, order):
    rank = jnp.zeros_like(dest)
    for bit in order:
        rank = rank * 2 + (dest // bit) % 2
    return rank


def blur_kernel(lists, affinity, scale, homes, along_y, along_z, out, own, place, ext, send_sem, recv_sem):
    planes, height, depth = affinity.shape[1:]
    n = lax.axis_size("xy")
    me = lax.axis_index("xy")
    part_id = lax.axis_index("parts")
    has_left, has_right = me > 0, me < n - 1
    left, right = (part_id, me - 1), (part_id, me + 1)
    barrier = pltpu.get_barrier_semaphore()

    for there, device in ((has_left, left), (has_right, right)):
        @pl.when(there)
        def _():
            pl.semaphore_signal(barrier, inc=1, device_id=device, device_id_type=MESH)
    for c in range(3):
        columns = jnp.transpose(scale[c], (1, 0))
        for p in range(planes):
            ext[c, HALO + p] = affinity[c, p].astype(jnp.float32) * columns[:, p:p + 1]

    inside = jnp.logical_and(has_left, has_right)

    @pl.when(inside)
    def _():
        pl.semaphore_wait(barrier, 2)

    @pl.when(jnp.logical_and(jnp.logical_not(inside), n > 1))
    def _():
        pl.semaphore_wait(barrier, 1)

    def to_right(p):
        return pltpu.make_async_remote_copy(
            src_ref=ext.at[:, HALO + p], dst_ref=ext.at[:, p],
            send_sem=send_sem.at[0, p], recv_sem=recv_sem.at[0, p],
            device_id=right, device_id_type=MESH)

    def to_left(p):
        return pltpu.make_async_remote_copy(
            src_ref=ext.at[:, HALO + p], dst_ref=ext.at[:, HALO + planes + p],
            send_sem=send_sem.at[1, p], recv_sem=recv_sem.at[1, p],
            device_id=left, device_id_type=MESH)

    @pl.when(has_right)
    def _():
        for p in reversed(range(planes)):
            to_right(p).start()

    @pl.when(has_left)
    def _():
        for p in range(planes):
            to_left(p).start()

    own[...] = ext[:, HALO:HALO + planes]
    rows = homes.shape[0]
    e_dev = rows * 128 // n
    parts = len(lists)
    tile = e_dev // (2 * parts)
    home = homes[...]
    dest, inner = home // e_dev, home % e_dev
    half, inner = inner // (parts * tile), inner % (parts * tile)
    part, row = inner // tile, inner % tile
    rank = jnp.where(part == 1, rank_of(dest, lists[1]), rank_of(dest, lists[0]))
    place[:rows, :] = ((part * n + rank) * 2 + half) * tile + row
    place[rows:, :] = jnp.full((8, 128), rows * 128, jnp.int32)

    @pl.when(jnp.logical_not(has_left))
    def _():
        ext[:, :HALO] = jnp.zeros((3, HALO, height, depth), jnp.float32)

    @pl.when(jnp.logical_not(has_right))
    def _():
        ext[:, HALO + planes:] = jnp.zeros((3, HALO, height, depth), jnp.float32)

    def need(low, high):
        @pl.when(has_left)
        def _():
            to_right(low).wait_recv()

        @pl.when(has_right)
        def _():
            to_left(high).wait_recv()

    middle = planes // 2
    for p in range(middle):
        need(planes - 1 - p, p)

    weights = [taps(s) for s in SIGMAS]

    @pl.loop(0, middle)
    def _(step):
        need(middle - 1 - step, middle + step)
        for q in (middle - 1 - step, middle + step):
            crossed = [[] for _ in SIGMAS]
            for c in range(3):
                chunks = [[] for _ in SIGMAS]
                for z in range(0, height, 16):
                    mid = ext[c, q + HALO, z:z + 16, :]
                    acc = [mid * float(w[HALO]) for w in weights]
                    for t in range(1, HALO + 1):
                        both = ext[c, q + HALO - t, z:z + 16, :] + ext[c, q + HALO + t, z:z + 16, :]
                        acc = [a + both * float(w[HALO + t]) for a, w in zip(acc, weights)]
                    for i in range(4):
                        chunks[i].append(acc[i])
                for i in range(4):
                    crossed[i].append(jnp.concatenate(chunks[i], 0))
            for i in range(4):
                high, low = split(jnp.concatenate(crossed[i], 0))
                wide = jnp.dot(jnp.concatenate([high, low], 1), along_y[i], preferred_element_type=jnp.float32)
                field = wide[:, :depth] + wide[:, depth:]
                high, low = split(field)
                highs = jnp.concatenate([high[c * height:(c + 1) * height] for c in range(3)], 1)
                lows = jnp.concatenate([low[c * height:(c + 1) * height] for c in range(3)], 1)
                stacked = jnp.concatenate([highs, lows, highs, lows], 0)
                done = jnp.dot(along_z[i], stacked, preferred_element_type=jnp.float32)
                for c in range(3):
                    out[q, 3 * i + c] = done[:, c * depth:(c + 1) * depth]

    @pl.when(has_right)
    def _():
        for p in range(planes):
            to_right(p).wait_send()

    @pl.when(has_left)
    def _():
        for p in range(planes):
            to_left(p).wait_send()


def sums_kernel(planes, banks, own, resp, slots, elist, place, out, rows, *tables):
    q = pl.program_id(0)
    height = own.shape[2]

    def add_rows(base):
        for e in range(128):
            at = place[elist[base + e]]
            table = tables[e % banks]
            table[pl.ds(at, 1), :] += rows[e:e + 1, :]

    @pl.when(q == 0)
    def _():
        rows[...] = jnp.zeros_like(rows)
        for table in tables:
            @pl.loop(0, table.shape[0] // 64)
            def _(r):
                table[pl.ds(pl.multiple_of(r * 64, 64), 64), :] = jnp.zeros((64, 128), jnp.float32)

    slot_row = lax.broadcasted_iota(jnp.int32, (SLOTS, 128), 0)
    lane = lax.broadcasted_iota(jnp.int32, (8, 128), 1)
    lane_z = (lane // SLOTS) % 8
    spread = (lax.broadcasted_iota(jnp.int32, (8, 128), 0) + 8 - lane_z) % 8

    @pl.loop(0, height // 16)
    def _(j):
        add_rows(jnp.maximum(q * (height * SLOTS) + j * 128 - 128, 0))
        z16 = pl.multiple_of(j * 16, 16)
        slot = slots[0, pl.ds(z16, 16), :]
        hot = jnp.concatenate([
            (jnp.broadcast_to(slot[k:k + 1, :], (SLOTS, 128)) == slot_row).astype(jnp.float32) for k in range(16)
        ], 0).astype(jnp.bfloat16)
        rhs = jnp.concatenate([hot, hot], 1)
        groups = []
        for g in range(2):
            z0 = pl.multiple_of(j * 16 + g * 8, 8)
            r = [resp[0, k, pl.ds(z0, 8), :] for k in range(12)]
            raw = [own[c, 0, pl.ds(z0, 8), :] for c in range(3)]
            square = [a * a for a in r]
            cube = [a * b for a, b in zip(square, r)]
            fourth = [a * a for a in square]
            pairs = []
            for i in range(4):
                a, b, c = r[3 * i:3 * i + 3]
                pairs += [a * b, a * c, b * c]
            ones = [jnp.ones((8, 128), jnp.float32)]
            groups.append(r + square + cube + fourth + pairs + raw + ones)
        pieces = []
        for f in range(0, FEAT, 8):
            feats = jnp.concatenate(groups[0][f:f + 8] + groups[1][f:f + 8], 0)
            high, low = split(feats)
            lhs = jnp.concatenate([high, low], 1)
            prod = lax.dot_general(lhs, rhs, (((1,), (1,)), ((), ())), preferred_element_type=jnp.float32)
            piece = None
            for k in range(8):
                both = jnp.where(lane < 64, prod[k * 8:k * 8 + 8], prod[64 + k * 8:64 + k * 8 + 8])
                piece = both if k == 0 else jnp.where(spread == k, pltpu.roll(both, k, 0), piece)
            for bit in (1, 2, 4):
                piece = jnp.where((lane_z // bit) % 2 == 1, pltpu.roll(piece, 8 - bit, 0), piece)
            pieces.append(piece)
        block = jnp.concatenate(pieces, 0)
        rows[...] = jnp.transpose(jnp.concatenate([block, jnp.zeros_like(block)], 0), (1, 0))

    @pl.when(q == pl.num_programs(0) - 1)
    def _():
        add_rows(planes * height * SLOTS - 128)
        tile = out.shape[2]
        low_lane = lax.broadcasted_iota(jnp.int32, (tile, 128), 1) < FEAT

        @pl.loop(0, out.shape[0] * out.shape[1])
        def _(b):
            def total(start):
                at = pl.ds(pl.multiple_of(start, 8), tile)
                value = tables[0][at, :]
                for table in tables[1:]:
                    value = value + table[at, :]
                return value
            first = total(b * 2 * tile)
            second = total(b * 2 * tile + tile)
            second = pltpu.roll(second, FEAT, 1)
            out[b // out.shape[1], b % out.shape[1]] = jnp.where(low_lane, first, second)


def reduce_kernel(n, lists, table, out, *scratch):
    count = n.bit_length() - 1
    recv = scratch[:count]
    acc = scratch[count:2 * count]
    send_sem, recv_sem = scratch[2 * count:]
    me = lax.axis_index("xy")
    part_id = lax.axis_index("parts")

    def partner(bit):
        return me + bit * (1 - 2 * ((me // bit) % 2))

    barrier = pltpu.get_barrier_semaphore()
    for bit in bits_of(n):
        pl.semaphore_signal(barrier, inc=1, device_id=(part_id, partner(bit)), device_id_type=MESH)
    pl.semaphore_wait(barrier, count)

    copies = {}

    def start(p, k):
        bit = lists[p][k]
        size = n >> (k + 1)
        mine = (me // bit) % 2
        source = table.at[p] if k == 0 else acc[k - 1].at[p]
        copy = pltpu.make_async_remote_copy(
            src_ref=source.at[pl.ds((1 - mine) * size, size)],
            dst_ref=recv[k].at[p],
            send_sem=send_sem.at[p, k],
            recv_sem=recv_sem.at[p, k],
            device_id=(part_id, partner(bit)),
            device_id_type=MESH,
        )
        copy.start()
        copies[p, k] = copy

    def finish(p, k):
        bit = lists[p][k]
        size = n >> (k + 1)
        mine = (me // bit) % 2
        source = table.at[p] if k == 0 else acc[k - 1].at[p]
        copies[p, k].wait_recv()
        if k == count - 1:
            out[p] = source[mine] + recv[k][p, 0]
        else:
            acc[k][p] = source[pl.ds(mine * size, size)] + recv[k][p]

    for p in range(len(lists)):
        start(p, 0)
    for k in range(count):
        for p in range(len(lists)):
            finish(p, k)
            if k + 1 < count:
                start(p, k + 1)
    for copy in copies.values():
        copy.wait_send()


def finalize(table):
    count = table[:, FEAT - 1:]
    means = table[:, :FEAT - 1] / jnp.maximum(count, 1.0)
    return jnp.concatenate([means, jnp.log1p(count)], 1)


def shards(affinity, block_scale, slot_map, edge_list, valid_count, edge_home):
    planes, height, depth = affinity.shape[1:]
    n = lax.axis_size("xy")
    edges = edge_home.shape[0]
    e_dev = edges // n
    lists = orders(n)
    parts = len(lists)
    tile = e_dev // (2 * parts)
    valid = jnp.arange(SLOTS, dtype=jnp.int32) < valid_count[..., None]
    elist = jnp.where(valid, edge_list, edges).reshape(-1)

    ys, zs = [], []
    for sigma in SIGMAS:
        high, low = band(sigma, depth)
        ys.append(np.block([[high, low], [high, low]]))
        high, low = band(sigma, height)
        zs.append(np.concatenate([high, high, low, low], 1))
    along_y = jnp.asarray(np.stack(ys), jnp.bfloat16)
    along_z = jnp.asarray(np.stack(zs), jnp.bfloat16)
    banks = 4 if edges * 512 * 4 <= (24 << 20) else 1
    whole = pl.BlockSpec(memory_space=VMEM)
    smem = pl.BlockSpec(memory_space=pltpu.SMEM)
    resp, dequant, place = pl.pallas_call(
        functools.partial(blur_kernel, lists),
        out_shape=[
            jax.ShapeDtypeStruct((planes, 12, height, depth), jnp.float32),
            jax.ShapeDtypeStruct((3, planes, height, depth), jnp.float32),
            jax.ShapeDtypeStruct((edges // 128 + 8, 128), jnp.int32),
        ],
        in_specs=[whole] * 5,
        out_specs=[whole] * 3,
        scratch_shapes=[
            VMEM((3, planes + 2 * HALO, height, depth), jnp.float32),
            pltpu.SemaphoreType.DMA((2, planes)),
            pltpu.SemaphoreType.DMA((2, planes)),
        ],
        compiler_params=pltpu.CompilerParams(collective_id=1, has_side_effects=True, vmem_limit_bytes=56 << 20),
    )(affinity, block_scale, edge_home.reshape(edges // 128, 128), along_y, along_z)
    table = pl.pallas_call(
        functools.partial(sums_kernel, planes, banks),
        grid=(planes,),
        out_shape=jax.ShapeDtypeStruct((parts, n, tile, 128), jnp.float32),
        in_specs=[
            pl.BlockSpec((3, 1, height, depth), lambda q: (0, q, 0, 0)),
            pl.BlockSpec((1, 12, height, depth), lambda q: (q, 0, 0, 0)),
            pl.BlockSpec((1, height, depth), lambda q: (q, 0, 0)),
            smem, smem,
        ],
        out_specs=whole,
        scratch_shapes=[
            VMEM((128, 128), jnp.float32),
        ] + [VMEM((edges + 64, 128), jnp.float32)] * banks,
        compiler_params=pltpu.CompilerParams(vmem_limit_bytes=56 << 20),
    )(dequant, resp, slot_map, elist, place.reshape(-1))

    count = n.bit_length() - 1
    sizes = [n >> (k + 1) for k in range(count)]
    total = pl.pallas_call(
        functools.partial(reduce_kernel, n, lists),
        out_shape=jax.ShapeDtypeStruct((parts, tile, 128), jnp.float32),
        in_specs=[whole],
        out_specs=whole,
        scratch_shapes=[VMEM((parts, s, tile, 128), jnp.float32) for s in sizes] * 2 + [
            pltpu.SemaphoreType.DMA((parts, count)),
            pltpu.SemaphoreType.DMA((parts, count)),
        ],
        compiler_params=pltpu.CompilerParams(collective_id=0, has_side_effects=True, vmem_limit_bytes=56 << 20),
    )(table)
    total = total.reshape(parts * tile, 128)
    return finalize(jnp.concatenate([total[:, :FEAT], total[:, FEAT:]], 0))


def solution(mesh):
    in_specs = (
        P(None, ("parts", "xy"), None, None),
        P(None, ("parts", "xy"), None),
        P(("parts", "xy"), None, None),
        P(("parts", "xy"), None, None),
        P(("parts", "xy"), None),
        P("parts"),
    )
    out_specs = P(("parts", "xy"), None)
    return jax.shard_map(shards, mesh=mesh, in_specs=in_specs, out_specs=out_specs, check_vma=False)
```

```python
import functools
import math
import ml_dtypes
import numpy as np
import jax
import jax.numpy as jnp
from jax import lax
from jax.experimental import pallas as pl
from jax.experimental.pallas import tpu as pltpu
from jax.sharding import PartitionSpec as P

SLOTS = 8
HALO = 8
FEAT = 64
SIGMAS = (0.8, 1.3, 2.0, 3.0)
MESH = pl.DeviceIdType.MESH
VMEM = pltpu.VMEM


def taps(sigma):
    t = np.arange(-HALO, HALO + 1).astype(np.float64)
    w = np.exp(-t * t / (2.0 * sigma * sigma))
    return (w / w.sum()).astype(np.float32)


def band(sigma, length):
    w = taps(sigma)
    rows = np.arange(length)
    shift = rows[None, :] - rows[:, None] + HALO
    inside = (shift >= 0) & (shift <= 2 * HALO)
    full = np.where(inside, w[np.clip(shift, 0, 2 * HALO)], np.float32(0)).astype(np.float32)
    high = full.astype(ml_dtypes.bfloat16)
    low = (full - high.astype(np.float32)).astype(ml_dtypes.bfloat16)
    return high, low


def split(value):
    high = value.astype(jnp.bfloat16)
    low = (value - high.astype(jnp.float32)).astype(jnp.bfloat16)
    return high, low


def bits_of(n):
    return [1 << k for k in range(n.bit_length() - 1)]


def orders(n):
    bits = bits_of(n)
    late = bits[:1] + bits[2:] + bits[1:2]
    return (bits, late, bits, bits)


def rank_of(dest, order):
    rank = jnp.zeros_like(dest)
    for bit in order:
        rank = rank * 2 + (dest // bit) % 2
    return rank


def blur_kernel(lists, affinity, scale, homes, along_y, along_z, out, own, place, ext, send_sem, recv_sem):
    planes, height, depth = affinity.shape[1:]
    n = lax.axis_size("xy")
    me = lax.axis_index("xy")
    part_id = lax.axis_index("parts")
    has_left, has_right = me > 0, me < n - 1
    left, right = (part_id, me - 1), (part_id, me + 1)
    barrier = pltpu.get_barrier_semaphore()

    for there, device in ((has_left, left), (has_right, right)):
        @pl.when(there)
        def _():
            pl.semaphore_signal(barrier, inc=1, device_id=device, device_id_type=MESH)
    for c in range(3):
        columns = jnp.transpose(scale[c], (1, 0))
        for p in range(planes):
            ext[c, HALO + p] = affinity[c, p].astype(jnp.float32) * columns[:, p:p + 1]

    inside = jnp.logical_and(has_left, has_right)

    @pl.when(inside)
    def _():
        pl.semaphore_wait(barrier, 2)

    @pl.when(jnp.logical_and(jnp.logical_not(inside), n > 1))
    def _():
        pl.semaphore_wait(barrier, 1)

    def to_right(p):
        return pltpu.make_async_remote_copy(
            src_ref=ext.at[:, HALO + p], dst_ref=ext.at[:, p],
            send_sem=send_sem.at[0, p], recv_sem=recv_sem.at[0, p],
            device_id=right, device_id_type=MESH)

    def to_left(p):
        return pltpu.make_async_remote_copy(
            src_ref=ext.at[:, HALO + p], dst_ref=ext.at[:, HALO + planes + p],
            send_sem=send_sem.at[1, p], recv_sem=recv_sem.at[1, p],
            device_id=left, device_id_type=MESH)

    @pl.when(has_right)
    def _():
        for p in reversed(range(planes)):
            to_right(p).start()

    @pl.when(has_left)
    def _():
        for p in range(planes):
            to_left(p).start()

    own[...] = ext[:, HALO:HALO + planes]
    rows = homes.shape[0]
    e_dev = rows * 128 // n
    parts = len(lists)
    tile = e_dev // (2 * parts)
    home = homes[...]
    dest, inner = home // e_dev, home % e_dev
    half, inner = inner // (parts * tile), inner % (parts * tile)
    part, row = inner // tile, inner % tile
    rank = jnp.where(part == 1, rank_of(dest, lists[1]), rank_of(dest, lists[0]))
    place[:rows, :] = ((part * n + rank) * 2 + half) * tile + row
    place[rows:, :] = jnp.full((8, 128), rows * 128, jnp.int32)

    @pl.when(jnp.logical_not(has_left))
    def _():
        ext[:, :HALO] = jnp.zeros((3, HALO, height, depth), jnp.float32)

    @pl.when(jnp.logical_not(has_right))
    def _():
        ext[:, HALO + planes:] = jnp.zeros((3, HALO, height, depth), jnp.float32)

    side = me % 2
    even, odd = side == 0, side == 1

    @pl.when(jnp.logical_and(even, has_right))
    def _():
        for p in range(planes):
            to_left(p).wait_recv()

    @pl.when(jnp.logical_and(odd, has_left))
    def _():
        for p in range(planes):
            to_right(p).wait_recv()

    weights = [taps(s) for s in SIGMAS]

    @pl.loop(0, planes)
    def _(step):
        @pl.when(jnp.logical_and(even, has_left))
        def _():
            to_right(planes - 1 - step).wait_recv()

        @pl.when(jnp.logical_and(odd, has_right))
        def _():
            to_left(step).wait_recv()

        q = step + (1 - side) * (planes - 1 - 2 * step)
        crossed = [[] for _ in SIGMAS]
        for c in range(3):
            chunks = [[] for _ in SIGMAS]
            for z in range(0, height, 16):
                mid = ext[c, q + HALO, z:z + 16, :]
                acc = [mid * float(w[HALO]) for w in weights]
                for t in range(1, HALO + 1):
                    both = ext[c, q + HALO - t, z:z + 16, :] + ext[c, q + HALO + t, z:z + 16, :]
                    acc = [a + both * float(w[HALO + t]) for a, w in zip(acc, weights)]
                for i in range(4):
                    chunks[i].append(acc[i])
            for i in range(4):
                crossed[i].append(jnp.concatenate(chunks[i], 0))
        for i in range(4):
            high, low = split(jnp.concatenate(crossed[i], 0))
            wide = jnp.dot(jnp.concatenate([high, low], 1), along_y[i], preferred_element_type=jnp.float32)
            field = wide[:, :depth] + wide[:, depth:]
            high, low = split(field)
            highs = jnp.concatenate([high[c * height:(c + 1) * height] for c in range(3)], 1)
            lows = jnp.concatenate([low[c * height:(c + 1) * height] for c in range(3)], 1)
            stacked = jnp.concatenate([highs, lows, highs, lows], 0)
            done = jnp.dot(along_z[i], stacked, preferred_element_type=jnp.float32)
            for c in range(3):
                out[q, 3 * i + c] = done[:, c * depth:(c + 1) * depth]

    @pl.when(has_right)
    def _():
        for p in range(planes):
            to_right(p).wait_send()

    @pl.when(has_left)
    def _():
        for p in range(planes):
            to_left(p).wait_send()


def sums_kernel(planes, banks, own, resp, slots, elist, place, out, rows, *tables):
    q = pl.program_id(0)
    height = own.shape[2]

    def add_rows(base):
        for e in range(0, 128, 2 * banks):
            ats = [place[elist[base + e + u]] for u in range(2 * banks)]
            own_rows = [rows[e + u:e + u + 1, :] for u in range(2 * banks)]
            held = [tables[u % banks][pl.ds(ats[u], 1), :] for u in range(2 * banks)]
            for u in range(banks):
                again = (ats[u] == ats[u + banks]).astype(jnp.float32)
                first = held[u] + own_rows[u]
                second = held[u + banks] + own_rows[u + banks] + own_rows[u] * again
                tables[u][pl.ds(ats[u], 1), :] = first
                tables[u][pl.ds(ats[u + banks], 1), :] = second

    @pl.when(q == 0)
    def _():
        rows[...] = jnp.zeros_like(rows)
        for table in tables:
            @pl.loop(0, table.shape[0] // 64)
            def _(r):
                table[pl.ds(pl.multiple_of(r * 64, 64), 64), :] = jnp.zeros((64, 128), jnp.float32)

    slot_row = lax.broadcasted_iota(jnp.int32, (SLOTS, 128), 0)
    lane = lax.broadcasted_iota(jnp.int32, (8, 128), 1)
    lane_z = (lane // SLOTS) % 8
    spread = (lax.broadcasted_iota(jnp.int32, (8, 128), 0) + 8 - lane_z) % 8

    @pl.loop(0, height // 16)
    def _(j):
        add_rows(jnp.maximum(q * (height * SLOTS) + j * 128 - 128, 0))
        z16 = pl.multiple_of(j * 16, 16)
        slot = slots[0, pl.ds(z16, 16), :]
        hot = jnp.concatenate([
            (jnp.broadcast_to(slot[k:k + 1, :], (SLOTS, 128)) == slot_row).astype(jnp.float32) for k in range(16)
        ], 0)
        hot = jnp.transpose(hot, (1, 0)).astype(jnp.bfloat16)
        rhs = jnp.concatenate([hot, hot], 0)
        groups = []
        for g in range(2):
            z0 = pl.multiple_of(j * 16 + g * 8, 8)
            r = [resp[0, k, pl.ds(z0, 8), :] for k in range(12)]
            raw = [own[c, 0, pl.ds(z0, 8), :] for c in range(3)]
            square = [a * a for a in r]
            cube = [a * b for a, b in zip(square, r)]
            fourth = [a * a for a in square]
            pairs = []
            for i in range(4):
                a, b, c = r[3 * i:3 * i + 3]
                pairs += [a * b, a * c, b * c]
            ones = [jnp.ones((8, 128), jnp.float32)]
            groups.append(r + square + cube + fourth + pairs + raw + ones)
        pieces = []
        for f in range(0, FEAT, 8):
            feats = jnp.concatenate(groups[0][f:f + 8] + groups[1][f:f + 8], 0)
            high, low = split(feats)
            lhs = jnp.concatenate([high, low], 1)
            prod = jnp.dot(lhs, rhs, preferred_element_type=jnp.float32)
            piece = None
            for k in range(8):
                both = jnp.where(lane < 64, prod[k * 8:k * 8 + 8], prod[64 + k * 8:64 + k * 8 + 8])
                piece = both if k == 0 else jnp.where(spread == k, pltpu.roll(both, k, 0), piece)
            for bit in (1, 2, 4):
                piece = jnp.where((lane_z // bit) % 2 == 1, pltpu.roll(piece, 8 - bit, 0), piece)
            pieces.append(piece)
        block = jnp.concatenate(pieces, 0)
        rows[...] = jnp.transpose(jnp.concatenate([block, jnp.zeros_like(block)], 0), (1, 0))

    @pl.when(q == pl.num_programs(0) - 1)
    def _():
        add_rows(planes * height * SLOTS - 128)
        tile = out.shape[2]
        low_lane = lax.broadcasted_iota(jnp.int32, (tile, 128), 1) < FEAT

        @pl.loop(0, out.shape[0] * out.shape[1])
        def _(b):
            def total(start):
                at = pl.ds(pl.multiple_of(start, 8), tile)
                value = tables[0][at, :]
                for table in tables[1:]:
                    value = value + table[at, :]
                return value
            first = total(b * 2 * tile)
            second = total(b * 2 * tile + tile)
            second = pltpu.roll(second, FEAT, 1)
            out[b // out.shape[1], b % out.shape[1]] = jnp.where(low_lane, first, second)


def reduce_kernel(n, lists, table, out, *scratch):
    count = n.bit_length() - 1
    recv = scratch[:count]
    acc = scratch[count:2 * count]
    send_sem, recv_sem = scratch[2 * count:]
    me = lax.axis_index("xy")
    part_id = lax.axis_index("parts")

    def partner(bit):
        return me + bit * (1 - 2 * ((me // bit) % 2))

    barrier = pltpu.get_barrier_semaphore()
    for bit in bits_of(n):
        pl.semaphore_signal(barrier, inc=1, device_id=(part_id, partner(bit)), device_id_type=MESH)
    pl.semaphore_wait(barrier, count)

    copies = {}

    def start(p, k):
        bit = lists[p][k]
        size = n >> (k + 1)
        mine = (me // bit) % 2
        source = table.at[p] if k == 0 else acc[k - 1].at[p]
        copy = pltpu.make_async_remote_copy(
            src_ref=source.at[pl.ds((1 - mine) * size, size)],
            dst_ref=recv[k].at[p],
            send_sem=send_sem.at[p, k],
            recv_sem=recv_sem.at[p, k],
            device_id=(part_id, partner(bit)),
            device_id_type=MESH,
        )
        copy.start()
        copies[p, k] = copy

    def finish(p, k):
        bit = lists[p][k]
        size = n >> (k + 1)
        mine = (me // bit) % 2
        source = table.at[p] if k == 0 else acc[k - 1].at[p]
        copies[p, k].wait_recv()
        if k == count - 1:
            out[p] = source[mine] + recv[k][p, 0]
        else:
            acc[k][p] = source[pl.ds(mine * size, size)] + recv[k][p]

    for p in range(len(lists)):
        start(p, 0)
    for k in range(count):
        for p in range(len(lists)):
            finish(p, k)
            if k + 1 < count:
                start(p, k + 1)
    for copy in copies.values():
        copy.wait_send()


def finalize(table):
    count = table[:, FEAT - 1:]
    means = table[:, :FEAT - 1] / jnp.maximum(count, 1.0)
    return jnp.concatenate([means, jnp.log1p(count)], 1)


def shards(affinity, block_scale, slot_map, edge_list, valid_count, edge_home):
    planes, height, depth = affinity.shape[1:]
    n = lax.axis_size("xy")
    edges = edge_home.shape[0]
    e_dev = edges // n
    lists = orders(n)
    parts = len(lists)
    tile = e_dev // (2 * parts)
    valid = jnp.arange(SLOTS, dtype=jnp.int32) < valid_count[..., None]
    elist = jnp.where(valid, edge_list, edges).reshape(-1)

    ys, zs = [], []
    for sigma in SIGMAS:
        high, low = band(sigma, depth)
        ys.append(np.block([[high, low], [high, low]]))
        high, low = band(sigma, height)
        zs.append(np.concatenate([high, high, low, low], 1))
    along_y = jnp.asarray(np.stack(ys), jnp.bfloat16)
    along_z = jnp.asarray(np.stack(zs), jnp.bfloat16)
    banks = 4 if edges * 512 * 4 <= (24 << 20) else 1
    whole = pl.BlockSpec(memory_space=VMEM)
    smem = pl.BlockSpec(memory_space=pltpu.SMEM)
    resp, dequant, place = pl.pallas_call(
        functools.partial(blur_kernel, lists),
        out_shape=[
            jax.ShapeDtypeStruct((planes, 12, height, depth), jnp.float32),
            jax.ShapeDtypeStruct((3, planes, height, depth), jnp.float32),
            jax.ShapeDtypeStruct((edges // 128 + 8, 128), jnp.int32),
        ],
        in_specs=[whole] * 5,
        out_specs=[whole] * 3,
        scratch_shapes=[
            VMEM((3, planes + 2 * HALO, height, depth), jnp.float32),
            pltpu.SemaphoreType.DMA((2, planes)),
            pltpu.SemaphoreType.DMA((2, planes)),
        ],
        compiler_params=pltpu.CompilerParams(collective_id=1, has_side_effects=True, vmem_limit_bytes=56 << 20),
    )(affinity, block_scale, edge_home.reshape(edges // 128, 128), along_y, along_z)
    table = pl.pallas_call(
        functools.partial(sums_kernel, planes, banks),
        grid=(planes,),
        out_shape=jax.ShapeDtypeStruct((parts, n, tile, 128), jnp.float32),
        in_specs=[
            pl.BlockSpec((3, 1, height, depth), lambda q: (0, q, 0, 0)),
            pl.BlockSpec((1, 12, height, depth), lambda q: (q, 0, 0, 0)),
            pl.BlockSpec((1, height, depth), lambda q: (q, 0, 0)),
            smem, smem,
        ],
        out_specs=whole,
        scratch_shapes=[
            VMEM((128, 128), jnp.float32),
        ] + [VMEM((edges + 64, 128), jnp.float32)] * banks,
        compiler_params=pltpu.CompilerParams(vmem_limit_bytes=56 << 20),
    )(dequant, resp, slot_map, elist, place.reshape(-1))

    count = n.bit_length() - 1
    sizes = [n >> (k + 1) for k in range(count)]
    total = pl.pallas_call(
        functools.partial(reduce_kernel, n, lists),
        out_shape=jax.ShapeDtypeStruct((parts, tile, 128), jnp.float32),
        in_specs=[whole],
        out_specs=whole,
        scratch_shapes=[VMEM((parts, s, tile, 128), jnp.float32) for s in sizes] * 2 + [
            pltpu.SemaphoreType.DMA((parts, count)),
            pltpu.SemaphoreType.DMA((parts, count)),
        ],
        compiler_params=pltpu.CompilerParams(collective_id=0, has_side_effects=True, vmem_limit_bytes=56 << 20),
    )(table)
    total = total.reshape(parts * tile, 128)
    return finalize(jnp.concatenate([total[:, :FEAT], total[:, FEAT:]], 0))


def solution(mesh):
    in_specs = (
        P(None, ("parts", "xy"), None, None),
        P(None, ("parts", "xy"), None),
        P(("parts", "xy"), None, None),
        P(("parts", "xy"), None, None),
        P(("parts", "xy"), None),
        P("parts"),
    )
    out_specs = P(("parts", "xy"), None)
    return jax.shard_map(shards, mesh=mesh, in_specs=in_specs, out_specs=out_specs, check_vma=False)
```

```python
import functools
import math
import ml_dtypes
import numpy as np
import jax
import jax.numpy as jnp
from jax import lax
from jax.experimental import pallas as pl
from jax.experimental.pallas import tpu as pltpu
from jax.sharding import PartitionSpec as P

SLOTS = 8
HALO = 8
FEAT = 64
SIGMAS = (0.8, 1.3, 2.0, 3.0)
MESH = pl.DeviceIdType.MESH
VMEM = pltpu.VMEM


def taps(sigma):
    t = np.arange(-HALO, HALO + 1).astype(np.float64)
    w = np.exp(-t * t / (2.0 * sigma * sigma))
    return (w / w.sum()).astype(np.float32)


def band(sigma, length):
    w = taps(sigma)
    rows = np.arange(length)
    shift = rows[None, :] - rows[:, None] + HALO
    inside = (shift >= 0) & (shift <= 2 * HALO)
    full = np.where(inside, w[np.clip(shift, 0, 2 * HALO)], np.float32(0)).astype(np.float32)
    high = full.astype(ml_dtypes.bfloat16)
    low = (full - high.astype(np.float32)).astype(ml_dtypes.bfloat16)
    return high, low


def split(value):
    high = value.astype(jnp.bfloat16)
    low = (value - high.astype(jnp.float32)).astype(jnp.bfloat16)
    return high, low


def bits_of(n):
    return [1 << k for k in range(n.bit_length() - 1)]


def orders(n):
    bits = bits_of(n)
    late = bits[:1] + bits[2:] + bits[1:2]
    return (bits, late, bits, bits)


def rank_of(dest, order):
    rank = jnp.zeros_like(dest)
    for bit in order:
        rank = rank * 2 + (dest // bit) % 2
    return rank


def blur_kernel(lists, affinity, scale, homes, along_y, along_z, out, own, place, ext, send_sem, recv_sem):
    planes, height, depth = affinity.shape[1:]
    n = lax.axis_size("xy")
    me = lax.axis_index("xy")
    part_id = lax.axis_index("parts")
    has_left, has_right = me > 0, me < n - 1
    left, right = (part_id, me - 1), (part_id, me + 1)
    barrier = pltpu.get_barrier_semaphore()

    for there, device in ((has_left, left), (has_right, right)):
        @pl.when(there)
        def _():
            pl.semaphore_signal(barrier, inc=1, device_id=device, device_id_type=MESH)
    for c in range(3):
        columns = jnp.transpose(scale[c], (1, 0))
        for p in range(planes):
            ext[c, HALO + p] = affinity[c, p].astype(jnp.float32) * columns[:, p:p + 1]

    inside = jnp.logical_and(has_left, has_right)

    @pl.when(inside)
    def _():
        pl.semaphore_wait(barrier, 2)

    @pl.when(jnp.logical_and(jnp.logical_not(inside), n > 1))
    def _():
        pl.semaphore_wait(barrier, 1)

    def to_right(p):
        return pltpu.make_async_remote_copy(
            src_ref=ext.at[:, HALO + p], dst_ref=ext.at[:, p],
            send_sem=send_sem.at[0, p], recv_sem=recv_sem.at[0, p],
            device_id=right, device_id_type=MESH)

    def to_left(p):
        return pltpu.make_async_remote_copy(
            src_ref=ext.at[:, HALO + p], dst_ref=ext.at[:, HALO + planes + p],
            send_sem=send_sem.at[1, p], recv_sem=recv_sem.at[1, p],
            device_id=left, device_id_type=MESH)

    @pl.when(has_right)
    def _():
        for p in reversed(range(planes)):
            to_right(p).start()

    @pl.when(has_left)
    def _():
        for p in range(planes):
            to_left(p).start()

    own[...] = ext[:, HALO:HALO + planes]
    rows = homes.shape[0]
    e_dev = rows * 128 // n
    parts = len(lists)
    tile = e_dev // (2 * parts)
    home = homes[...]
    dest, inner = home // e_dev, home % e_dev
    half, inner = inner // (parts * tile), inner % (parts * tile)
    part, row = inner // tile, inner % tile
    rank = jnp.where(part == 1, rank_of(dest, lists[1]), rank_of(dest, lists[0]))
    place[:rows, :] = ((part * n + rank) * 2 + half) * tile + row
    place[rows:, :] = jnp.full((8, 128), rows * 128, jnp.int32)

    @pl.when(jnp.logical_not(has_left))
    def _():
        ext[:, :HALO] = jnp.zeros((3, HALO, height, depth), jnp.float32)

    @pl.when(jnp.logical_not(has_right))
    def _():
        ext[:, HALO + planes:] = jnp.zeros((3, HALO, height, depth), jnp.float32)

    side = me % 2
    even, odd = side == 0, side == 1

    @pl.when(jnp.logical_and(even, has_right))
    def _():
        for p in range(planes):
            to_left(p).wait_recv()

    @pl.when(jnp.logical_and(odd, has_left))
    def _():
        for p in range(planes):
            to_right(p).wait_recv()

    weights = [taps(s) for s in SIGMAS]

    @pl.loop(0, planes)
    def _(step):
        @pl.when(jnp.logical_and(even, has_left))
        def _():
            to_right(planes - 1 - step).wait_recv()

        @pl.when(jnp.logical_and(odd, has_right))
        def _():
            to_left(step).wait_recv()

        q = step + (1 - side) * (planes - 1 - 2 * step)
        crossed = [[] for _ in SIGMAS]
        for c in range(3):
            chunks = [[] for _ in SIGMAS]
            for z in range(0, height, 16):
                mid = ext[c, q + HALO, z:z + 16, :]
                acc = [mid * float(w[HALO]) for w in weights]
                for t in range(1, HALO + 1):
                    both = ext[c, q + HALO - t, z:z + 16, :] + ext[c, q + HALO + t, z:z + 16, :]
                    acc = [a + both * float(w[HALO + t]) for a, w in zip(acc, weights)]
                for i in range(4):
                    chunks[i].append(acc[i])
            for i in range(4):
                crossed[i].append(jnp.concatenate(chunks[i], 0))
        for i in range(4):
            high, low = split(jnp.concatenate(crossed[i], 0))
            wide = jnp.dot(jnp.concatenate([high, low], 1), along_y[i], preferred_element_type=jnp.float32)
            field = wide[:, :depth] + wide[:, depth:]
            high, low = split(field)
            highs = jnp.concatenate([high[c * height:(c + 1) * height] for c in range(3)], 1)
            lows = jnp.concatenate([low[c * height:(c + 1) * height] for c in range(3)], 1)
            stacked = jnp.concatenate([highs, lows, highs, lows], 0)
            done = jnp.dot(along_z[i], stacked, preferred_element_type=jnp.float32)
            for c in range(3):
                out[q, 3 * i + c] = done[:, c * depth:(c + 1) * depth]

    @pl.when(has_right)
    def _():
        for p in range(planes):
            to_right(p).wait_send()

    @pl.when(has_left)
    def _():
        for p in range(planes):
            to_left(p).wait_send()


def sums_kernel(planes, banks, own, resp, slots, elist, place, out, rows, *tables):
    q = pl.program_id(0)
    height = own.shape[2]

    def add_rows(base):
        for e in range(128):
            at = place[elist[base + e]]
            table = tables[e % banks]
            table[pl.ds(at, 1), :] += rows[e:e + 1, :]

    @pl.when(q == 0)
    def _():
        rows[...] = jnp.zeros_like(rows)
        for table in tables:
            @pl.loop(0, table.shape[0] // 64)
            def _(r):
                table[pl.ds(pl.multiple_of(r * 64, 64), 64), :] = jnp.zeros((64, 128), jnp.float32)

    slot_row = lax.broadcasted_iota(jnp.int32, (SLOTS, 128), 0)
    lane = lax.broadcasted_iota(jnp.int32, (8, 128), 1)
    lane_z = (lane // SLOTS) % 8
    spread = (lax.broadcasted_iota(jnp.int32, (8, 128), 0) + 8 - lane_z) % 8

    @pl.loop(0, height // 16)
    def _(j):
        add_rows(jnp.maximum(q * (height * SLOTS) + j * 128 - 128, 0))
        z16 = pl.multiple_of(j * 16, 16)
        slot = slots[0, pl.ds(z16, 16), :]
        hot = jnp.concatenate([
            (jnp.broadcast_to(slot[k:k + 1, :], (SLOTS, 128)) == slot_row).astype(jnp.float32) for k in range(16)
        ], 0).astype(jnp.bfloat16)
        rhs = jnp.concatenate([hot, hot], 1)
        groups = []
        for g in range(2):
            z0 = pl.multiple_of(j * 16 + g * 8, 8)
            r = [resp[0, k, pl.ds(z0, 8), :] for k in range(12)]
            raw = [own[c, 0, pl.ds(z0, 8), :] for c in range(3)]
            square = [a * a for a in r]
            cube = [a * b for a, b in zip(square, r)]
            fourth = [a * a for a in square]
            pairs = []
            for i in range(4):
                a, b, c = r[3 * i:3 * i + 3]
                pairs += [a * b, a * c, b * c]
            ones = [jnp.ones((8, 128), jnp.float32)]
            groups.append(r + square + cube + fourth + pairs + raw + ones)
        pieces = []
        for f in range(0, FEAT, 8):
            feats = jnp.concatenate(groups[0][f:f + 8] + groups[1][f:f + 8], 0)
            high, low = split(feats)
            lhs = jnp.concatenate([high, low], 1)
            prod = lax.dot_general(lhs, rhs, (((1,), (1,)), ((), ())), preferred_element_type=jnp.float32)
            piece = None
            for k in range(8):
                both = jnp.where(lane < 64, prod[k * 8:k * 8 + 8], prod[64 + k * 8:64 + k * 8 + 8])
                piece = both if k == 0 else jnp.where(spread == k, pltpu.roll(both, k, 0), piece)
            for bit in (1, 2, 4):
                piece = jnp.where((lane_z // bit) % 2 == 1, pltpu.roll(piece, 8 - bit, 0), piece)
            pieces.append(piece)
        block = jnp.concatenate(pieces, 0)
        rows[...] = jnp.transpose(jnp.concatenate([block, jnp.zeros_like(block)], 0), (1, 0))

    @pl.when(q == pl.num_programs(0) - 1)
    def _():
        add_rows(planes * height * SLOTS - 128)
        tile = out.shape[2]
        low_lane = lax.broadcasted_iota(jnp.int32, (tile, 128), 1) < FEAT

        @pl.loop(0, out.shape[0] * out.shape[1])
        def _(b):
            def total(start):
                at = pl.ds(pl.multiple_of(start, 8), tile)
                value = tables[0][at, :]
                for table in tables[1:]:
                    value = value + table[at, :]
                return value
            first = total(b * 2 * tile)
            second = total(b * 2 * tile + tile)
            second = pltpu.roll(second, FEAT, 1)
            out[b // out.shape[1], b % out.shape[1]] = jnp.where(low_lane, first, second)


def reduce_kernel(n, lists, table, out, *scratch):
    count = n.bit_length() - 1
    recv = scratch[:count]
    acc = scratch[count:2 * count]
    send_sem, recv_sem = scratch[2 * count:]
    me = lax.axis_index("xy")
    part_id = lax.axis_index("parts")

    def partner(bit):
        return me + bit * (1 - 2 * ((me // bit) % 2))

    barrier = pltpu.get_barrier_semaphore()
    for bit in bits_of(n):
        pl.semaphore_signal(barrier, inc=1, device_id=(part_id, partner(bit)), device_id_type=MESH)
    pl.semaphore_wait(barrier, count)

    copies = {}
    lane = lax.broadcasted_iota(jnp.int32, table.shape[2:], 1)

    def start(p, k):
        bit = lists[p][k]
        size = n >> (k + 1)
        mine = (me // bit) % 2
        source = table.at[p] if k == 0 else acc[k - 1].at[p]
        copy = pltpu.make_async_remote_copy(
            src_ref=source.at[pl.ds((1 - mine) * size, size)],
            dst_ref=recv[k].at[p],
            send_sem=send_sem.at[p, k],
            recv_sem=recv_sem.at[p, k],
            device_id=(part_id, partner(bit)),
            device_id_type=MESH,
        )
        copy.start()
        copies[p, k] = copy

    def finish(p, k):
        bit = lists[p][k]
        size = n >> (k + 1)
        mine = (me // bit) % 2
        source = table.at[p] if k == 0 else acc[k - 1].at[p]
        copies[p, k].wait_recv()
        if k == count - 1:
            total = source[mine] + recv[k][p, 0]
            tile = total.shape[0]
            last = (lane % FEAT) == FEAT - 1
            low = jnp.where(lane < FEAT, total[:, FEAT - 1:FEAT], total[:, 2 * FEAT - 1:])
            done = jnp.where(last, jnp.log1p(total), total / jnp.maximum(low, 1.0))
            out[p * tile:(p + 1) * tile, :] = done[:, :FEAT]
            base = (len(lists) + p) * tile
            out[base:base + tile, :] = done[:, FEAT:]
        else:
            acc[k][p] = source[pl.ds(mine * size, size)] + recv[k][p]

    for p in range(len(lists)):
        start(p, 0)
    for k in range(count):
        for p in range(len(lists)):
            finish(p, k)
            if k + 1 < count:
                start(p, k + 1)
    for copy in copies.values():
        copy.wait_send()


def shards(affinity, block_scale, slot_map, edge_list, valid_count, edge_home):
    planes, height, depth = affinity.shape[1:]
    n = lax.axis_size("xy")
    edges = edge_home.shape[0]
    e_dev = edges // n
    lists = orders(n)
    parts = len(lists)
    tile = e_dev // (2 * parts)
    valid = jnp.arange(SLOTS, dtype=jnp.int32) < valid_count[..., None]
    elist = jnp.where(valid, edge_list, edges).reshape(-1)

    ys, zs = [], []
    for sigma in SIGMAS:
        high, low = band(sigma, depth)
        ys.append(np.block([[high, low], [high, low]]))
        high, low = band(sigma, height)
        zs.append(np.concatenate([high, high, low, low], 1))
    along_y = jnp.asarray(np.stack(ys), jnp.bfloat16)
    along_z = jnp.asarray(np.stack(zs), jnp.bfloat16)
    banks = 2 if edges * 512 * 4 <= (24 << 20) else 1
    whole = pl.BlockSpec(memory_space=VMEM)
    smem = pl.BlockSpec(memory_space=pltpu.SMEM)
    resp, dequant, place = pl.pallas_call(
        functools.partial(blur_kernel, lists),
        out_shape=[
            jax.ShapeDtypeStruct((planes, 12, height, depth), jnp.float32),
            jax.ShapeDtypeStruct((3, planes, height, depth), jnp.float32),
            jax.ShapeDtypeStruct((edges // 128 + 8, 128), jnp.int32),
        ],
        in_specs=[whole] * 5,
        out_specs=[whole] * 3,
        scratch_shapes=[
            VMEM((3, planes + 2 * HALO, height, depth), jnp.float32),
            pltpu.SemaphoreType.DMA((2, planes)),
            pltpu.SemaphoreType.DMA((2, planes)),
        ],
        compiler_params=pltpu.CompilerParams(collective_id=1, has_side_effects=True, vmem_limit_bytes=56 << 20),
    )(affinity, block_scale, edge_home.reshape(edges // 128, 128), along_y, along_z)
    table = pl.pallas_call(
        functools.partial(sums_kernel, planes, banks),
        grid=(planes,),
        out_shape=jax.ShapeDtypeStruct((parts, n, tile, 128), jnp.float32),
        in_specs=[
            pl.BlockSpec((3, 1, height, depth), lambda q: (0, q, 0, 0)),
            pl.BlockSpec((1, 12, height, depth), lambda q: (q, 0, 0, 0)),
            pl.BlockSpec((1, height, depth), lambda q: (q, 0, 0)),
            smem, smem,
        ],
        out_specs=whole,
        scratch_shapes=[
            VMEM((128, 128), jnp.float32),
        ] + [VMEM((edges + 64, 128), jnp.float32)] * banks,
        compiler_params=pltpu.CompilerParams(vmem_limit_bytes=56 << 20),
    )(dequant, resp, slot_map, elist, place.reshape(-1))

    count = n.bit_length() - 1
    sizes = [n >> (k + 1) for k in range(count)]
    return pl.pallas_call(
        functools.partial(reduce_kernel, n, lists),
        out_shape=jax.ShapeDtypeStruct((e_dev, FEAT), jnp.float32),
        in_specs=[whole],
        out_specs=whole,
        scratch_shapes=[VMEM((parts, s, tile, 128), jnp.float32) for s in sizes] * 2 + [
            pltpu.SemaphoreType.DMA((parts, count)),
            pltpu.SemaphoreType.DMA((parts, count)),
        ],
        compiler_params=pltpu.CompilerParams(collective_id=0, has_side_effects=True, vmem_limit_bytes=56 << 20),
    )(table)


def solution(mesh):
    in_specs = (
        P(None, ("parts", "xy"), None, None),
        P(None, ("parts", "xy"), None),
        P(("parts", "xy"), None, None),
        P(("parts", "xy"), None, None),
        P(("parts", "xy"), None),
        P("parts"),
    )
    out_specs = P(("parts", "xy"), None)
    return jax.shard_map(shards, mesh=mesh, in_specs=in_specs, out_specs=out_specs, check_vma=False)
```

```python
import functools
import math
import ml_dtypes
import numpy as np
import jax
import jax.numpy as jnp
from jax import lax
from jax.experimental import pallas as pl
from jax.experimental.pallas import tpu as pltpu
from jax.sharding import PartitionSpec as P

SLOTS = 8
HALO = 8
FEAT = 64
SIGMAS = (0.8, 1.3, 2.0, 3.0)
MESH = pl.DeviceIdType.MESH
VMEM = pltpu.VMEM


def taps(sigma):
    t = np.arange(-HALO, HALO + 1).astype(np.float64)
    w = np.exp(-t * t / (2.0 * sigma * sigma))
    return (w / w.sum()).astype(np.float32)


def band(sigma, length):
    w = taps(sigma)
    rows = np.arange(length)
    shift = rows[None, :] - rows[:, None] + HALO
    inside = (shift >= 0) & (shift <= 2 * HALO)
    full = np.where(inside, w[np.clip(shift, 0, 2 * HALO)], np.float32(0)).astype(np.float32)
    high = full.astype(ml_dtypes.bfloat16)
    low = (full - high.astype(np.float32)).astype(ml_dtypes.bfloat16)
    return high, low


def split(value):
    high = value.astype(jnp.bfloat16)
    low = (value - high.astype(jnp.float32)).astype(jnp.bfloat16)
    return high, low


def bits_of(n):
    return [1 << k for k in range(n.bit_length() - 1)]


def orders(n):
    bits = bits_of(n)
    late = bits[:1] + bits[2:] + bits[1:2]
    return (bits, late, bits, bits)


def rank_of(dest, order):
    rank = jnp.zeros_like(dest)
    for bit in order:
        rank = rank * 2 + (dest // bit) % 2
    return rank


def blur_kernel(lists, affinity, scale, homes, along_y, along_z, out, own, place, ext, done_planes, send_sem, recv_sem, out_sem):
    planes, height, depth = affinity.shape[1:]
    n = lax.axis_size("xy")
    me = lax.axis_index("xy")
    part_id = lax.axis_index("parts")
    has_left, has_right = me > 0, me < n - 1
    left, right = (part_id, me - 1), (part_id, me + 1)
    barrier = pltpu.get_barrier_semaphore()

    for there, device in ((has_left, left), (has_right, right)):
        @pl.when(there)
        def _():
            pl.semaphore_signal(barrier, inc=1, device_id=device, device_id_type=MESH)
    for c in range(3):
        columns = jnp.transpose(scale[c], (1, 0))
        for p in range(planes):
            ext[c, HALO + p] = affinity[c, p].astype(jnp.float32) * columns[:, p:p + 1]

    inside = jnp.logical_and(has_left, has_right)

    @pl.when(inside)
    def _():
        pl.semaphore_wait(barrier, 2)

    @pl.when(jnp.logical_and(jnp.logical_not(inside), n > 1))
    def _():
        pl.semaphore_wait(barrier, 1)

    def to_right(p):
        return pltpu.make_async_remote_copy(
            src_ref=ext.at[:, HALO + p], dst_ref=ext.at[:, p],
            send_sem=send_sem.at[0, p], recv_sem=recv_sem.at[0, p],
            device_id=right, device_id_type=MESH)

    def to_left(p):
        return pltpu.make_async_remote_copy(
            src_ref=ext.at[:, HALO + p], dst_ref=ext.at[:, HALO + planes + p],
            send_sem=send_sem.at[1, p], recv_sem=recv_sem.at[1, p],
            device_id=left, device_id_type=MESH)

    side = me % 2
    even, odd = side == 0, side == 1

    def send_right(parity):
        @pl.when(jnp.logical_and(parity, has_right))
        def _():
            for p in reversed(range(planes)):
                to_right(p).start()

    def send_left(parity):
        @pl.when(jnp.logical_and(parity, has_left))
        def _():
            for p in range(planes):
                to_left(p).start()

    send_left(even)
    send_right(odd)
    send_right(even)
    send_left(odd)

    @pl.when(jnp.logical_not(has_left))
    def _():
        ext[:, :HALO] = jnp.zeros((3, HALO, height, depth), jnp.float32)

    @pl.when(jnp.logical_not(has_right))
    def _():
        ext[:, HALO + planes:] = jnp.zeros((3, HALO, height, depth), jnp.float32)

    own[...] = ext[:, HALO:HALO + planes]
    rows = homes.shape[0]
    e_dev = rows * 128 // n
    parts = len(lists)
    tile = e_dev // (2 * parts)
    home = homes[...]
    dest, inner = home // e_dev, home % e_dev
    half, inner = inner // (parts * tile), inner % (parts * tile)
    part, row = inner // tile, inner % tile
    rank = jnp.where(part == 1, rank_of(dest, lists[1]), rank_of(dest, lists[0]))
    place[:rows, :] = ((part * n + rank) * 2 + half) * tile + row
    place[rows:, :] = jnp.full((8, 128), rows * 128, jnp.int32)

    @pl.when(jnp.logical_and(even, has_right))
    def _():
        for p in range(planes):
            to_left(p).wait_recv()

    @pl.when(jnp.logical_and(odd, has_left))
    def _():
        for p in range(planes):
            to_right(p).wait_recv()

    weights = [taps(s) for s in SIGMAS]

    @pl.loop(0, planes)
    def _(step):
        @pl.when(jnp.logical_and(even, has_left))
        def _():
            to_right(planes - 1 - step).wait_recv()

        @pl.when(jnp.logical_and(odd, has_right))
        def _():
            to_left(step).wait_recv()

        q = step + (1 - side) * (planes - 1 - 2 * step)
        crossed = [[] for _ in SIGMAS]
        for c in range(3):
            chunks = [[] for _ in SIGMAS]
            for z in range(0, height, 16):
                mid = ext[c, q + HALO, z:z + 16, :]
                acc = [mid * float(w[HALO]) for w in weights]
                for t in range(1, HALO + 1):
                    both = ext[c, q + HALO - t, z:z + 16, :] + ext[c, q + HALO + t, z:z + 16, :]
                    acc = [a + both * float(w[HALO + t]) for a, w in zip(acc, weights)]
                for i in range(4):
                    chunks[i].append(acc[i])
            for i in range(4):
                crossed[i].append(jnp.concatenate(chunks[i], 0))
        for i in range(4):
            high, low = split(jnp.concatenate(crossed[i], 0))
            wide = jnp.dot(jnp.concatenate([high, low], 1), along_y[i], preferred_element_type=jnp.float32)
            field = wide[:, :depth] + wide[:, depth:]
            high, low = split(field)
            highs = jnp.concatenate([high[c * height:(c + 1) * height] for c in range(3)], 1)
            lows = jnp.concatenate([low[c * height:(c + 1) * height] for c in range(3)], 1)
            stacked = jnp.concatenate([highs, lows, highs, lows], 0)
            done = jnp.dot(along_z[i], stacked, preferred_element_type=jnp.float32)
            for c in range(3):
                done_planes[q, 3 * i + c] = done[:, c * depth:(c + 1) * depth]
        pltpu.make_async_copy(done_planes.at[q], out.at[q], out_sem.at[q]).start()

    for q in range(planes):
        pltpu.make_async_copy(done_planes.at[q], out.at[q], out_sem.at[q]).wait()

    @pl.when(has_right)
    def _():
        for p in range(planes):
            to_right(p).wait_send()

    @pl.when(has_left)
    def _():
        for p in range(planes):
            to_left(p).wait_send()


def sums_kernel(planes, banks, own, resp, slots, elist, place, out, rows, *tables):
    q = pl.program_id(0)
    height = own.shape[2]

    def add_rows(base):
        for e in range(128):
            at = place[elist[base + e]]
            table = tables[e % banks]
            table[pl.ds(at, 1), :] += rows[e:e + 1, :]

    @pl.when(q == 0)
    def _():
        rows[...] = jnp.zeros_like(rows)
        for table in tables:
            @pl.loop(0, table.shape[0] // 64)
            def _(r):
                table[pl.ds(pl.multiple_of(r * 64, 64), 64), :] = jnp.zeros((64, 128), jnp.float32)

    slot_row = lax.broadcasted_iota(jnp.int32, (SLOTS, 128), 0)
    lane = lax.broadcasted_iota(jnp.int32, (8, 128), 1)
    lane_z = (lane // SLOTS) % 8
    spread = (lax.broadcasted_iota(jnp.int32, (8, 128), 0) + 8 - lane_z) % 8

    @pl.loop(0, height // 16)
    def _(j):
        add_rows(jnp.maximum(q * (height * SLOTS) + j * 128 - 128, 0))
        z16 = pl.multiple_of(j * 16, 16)
        slot = slots[0, pl.ds(z16, 16), :]
        hot = jnp.concatenate([
            (jnp.broadcast_to(slot[k:k + 1, :], (SLOTS, 128)) == slot_row).astype(jnp.float32) for k in range(16)
        ], 0).astype(jnp.bfloat16)
        rhs = jnp.concatenate([hot, hot], 1)
        groups = []
        for g in range(2):
            z0 = pl.multiple_of(j * 16 + g * 8, 8)
            r = [resp[0, k, pl.ds(z0, 8), :] for k in range(12)]
            raw = [own[c, 0, pl.ds(z0, 8), :] for c in range(3)]
            square = [a * a for a in r]
            cube = [a * b for a, b in zip(square, r)]
            fourth = [a * a for a in square]
            pairs = []
            for i in range(4):
                a, b, c = r[3 * i:3 * i + 3]
                pairs += [a * b, a * c, b * c]
            ones = [jnp.ones((8, 128), jnp.float32)]
            groups.append(r + square + cube + fourth + pairs + raw + ones)
        pieces = []
        for f in range(0, FEAT, 8):
            feats = jnp.concatenate(groups[0][f:f + 8] + groups[1][f:f + 8], 0)
            high, low = split(feats)
            lhs = jnp.concatenate([high, low], 1)
            prod = lax.dot_general(lhs, rhs, (((1,), (1,)), ((), ())), preferred_element_type=jnp.float32)
            piece = None
            for k in range(8):
                both = jnp.where(lane < 64, prod[k * 8:k * 8 + 8], prod[64 + k * 8:64 + k * 8 + 8])
                piece = both if k == 0 else jnp.where(spread == k, pltpu.roll(both, k, 0), piece)
            for bit in (1, 2, 4):
                piece = jnp.where((lane_z // bit) % 2 == 1, pltpu.roll(piece, 8 - bit, 0), piece)
            pieces.append(piece)
        block = jnp.concatenate(pieces, 0)
        rows[...] = jnp.transpose(jnp.concatenate([block, jnp.zeros_like(block)], 0), (1, 0))

    @pl.when(q == pl.num_programs(0) - 1)
    def _():
        add_rows(planes * height * SLOTS - 128)
        tile = out.shape[2]
        low_lane = lax.broadcasted_iota(jnp.int32, (tile, 128), 1) < FEAT

        @pl.loop(0, out.shape[0] * out.shape[1])
        def _(b):
            def total(start):
                at = pl.ds(pl.multiple_of(start, 8), tile)
                value = tables[0][at, :]
                for table in tables[1:]:
                    value = value + table[at, :]
                return value
            first = total(b * 2 * tile)
            second = total(b * 2 * tile + tile)
            second = pltpu.roll(second, FEAT, 1)
            out[b // out.shape[1], b % out.shape[1]] = jnp.where(low_lane, first, second)


def reduce_kernel(n, lists, table, out, *scratch):
    count = n.bit_length() - 1
    recv = scratch[:count]
    acc = scratch[count:2 * count]
    send_sem, recv_sem = scratch[2 * count:]
    me = lax.axis_index("xy")
    part_id = lax.axis_index("parts")

    def partner(bit):
        return me + bit * (1 - 2 * ((me // bit) % 2))

    barrier = pltpu.get_barrier_semaphore()
    for bit in bits_of(n):
        pl.semaphore_signal(barrier, inc=1, device_id=(part_id, partner(bit)), device_id_type=MESH)
    pl.semaphore_wait(barrier, count)

    copies = {}
    lane = lax.broadcasted_iota(jnp.int32, table.shape[2:], 1)

    def start(p, k):
        bit = lists[p][k]
        size = n >> (k + 1)
        mine = (me // bit) % 2
        source = table.at[p] if k == 0 else acc[k - 1].at[p]
        copy = pltpu.make_async_remote_copy(
            src_ref=source.at[pl.ds((1 - mine) * size, size)],
            dst_ref=recv[k].at[p],
            send_sem=send_sem.at[p, k],
            recv_sem=recv_sem.at[p, k],
            device_id=(part_id, partner(bit)),
            device_id_type=MESH,
        )
        copy.start()
        copies[p, k] = copy

    def finish(p, k):
        bit = lists[p][k]
        size = n >> (k + 1)
        mine = (me // bit) % 2
        source = table.at[p] if k == 0 else acc[k - 1].at[p]
        copies[p, k].wait_recv()
        if k == count - 1:
            total = source[mine] + recv[k][p, 0]
            tile = total.shape[0]
            last = (lane % FEAT) == FEAT - 1
            low = jnp.where(lane < FEAT, total[:, FEAT - 1:FEAT], total[:, 2 * FEAT - 1:])
            done = jnp.where(last, jnp.log1p(total), total / jnp.maximum(low, 1.0))
            out[p * tile:(p + 1) * tile, :] = done[:, :FEAT]
            base = (len(lists) + p) * tile
            out[base:base + tile, :] = done[:, FEAT:]
        else:
            acc[k][p] = source[pl.ds(mine * size, size)] + recv[k][p]

    for p in range(len(lists)):
        start(p, 0)
    for k in range(count):
        for p in range(len(lists)):
            finish(p, k)
            if k + 1 < count:
                start(p, k + 1)
    for copy in copies.values():
        copy.wait_send()


def shards(affinity, block_scale, slot_map, edge_list, valid_count, edge_home):
    planes, height, depth = affinity.shape[1:]
    n = lax.axis_size("xy")
    edges = edge_home.shape[0]
    e_dev = edges // n
    lists = orders(n)
    parts = len(lists)
    tile = e_dev // (2 * parts)
    valid = jnp.arange(SLOTS, dtype=jnp.int32) < valid_count[..., None]
    elist = jnp.where(valid, edge_list, edges).reshape(-1)

    ys, zs = [], []
    for sigma in SIGMAS:
        high, low = band(sigma, depth)
        ys.append(np.block([[high, low], [high, low]]))
        high, low = band(sigma, height)
        zs.append(np.concatenate([high, high, low, low], 1))
    along_y = jnp.asarray(np.stack(ys), jnp.bfloat16)
    along_z = jnp.asarray(np.stack(zs), jnp.bfloat16)
    banks = 2 if edges * 512 * 4 <= (24 << 20) else 1
    whole = pl.BlockSpec(memory_space=VMEM)
    smem = pl.BlockSpec(memory_space=pltpu.SMEM)
    resp, dequant, place = pl.pallas_call(
        functools.partial(blur_kernel, lists),
        out_shape=[
            jax.ShapeDtypeStruct((planes, 12, height, depth), jnp.float32),
            jax.ShapeDtypeStruct((3, planes, height, depth), jnp.float32),
            jax.ShapeDtypeStruct((edges // 128 + 8, 128), jnp.int32),
        ],
        in_specs=[whole] * 5,
        out_specs=[pl.BlockSpec(memory_space=pl.ANY), whole, whole],
        scratch_shapes=[
            VMEM((3, planes + 2 * HALO, height, depth), jnp.float32),
            VMEM((planes, 12, height, depth), jnp.float32),
            pltpu.SemaphoreType.DMA((2, planes)),
            pltpu.SemaphoreType.DMA((2, planes)),
            pltpu.SemaphoreType.DMA((planes,)),
        ],
        compiler_params=pltpu.CompilerParams(collective_id=1, has_side_effects=True, vmem_limit_bytes=56 << 20),
    )(affinity, block_scale, edge_home.reshape(edges // 128, 128), along_y, along_z)
    table = pl.pallas_call(
        functools.partial(sums_kernel, planes, banks),
        grid=(planes,),
        out_shape=jax.ShapeDtypeStruct((parts, n, tile, 128), jnp.float32),
        in_specs=[
            pl.BlockSpec((3, 1, height, depth), lambda q: (0, q, 0, 0)),
            pl.BlockSpec((1, 12, height, depth), lambda q: (q, 0, 0, 0)),
            pl.BlockSpec((1, height, depth), lambda q: (q, 0, 0)),
            smem, smem,
        ],
        out_specs=whole,
        scratch_shapes=[
            VMEM((128, 128), jnp.float32),
        ] + [VMEM((edges + 64, 128), jnp.float32)] * banks,
        compiler_params=pltpu.CompilerParams(vmem_limit_bytes=56 << 20),
    )(dequant, resp, slot_map, elist, place.reshape(-1))

    count = n.bit_length() - 1
    sizes = [n >> (k + 1) for k in range(count)]
    return pl.pallas_call(
        functools.partial(reduce_kernel, n, lists),
        out_shape=jax.ShapeDtypeStruct((e_dev, FEAT), jnp.float32),
        in_specs=[whole],
        out_specs=whole,
        scratch_shapes=[VMEM((parts, s, tile, 128), jnp.float32) for s in sizes] * 2 + [
            pltpu.SemaphoreType.DMA((parts, count)),
            pltpu.SemaphoreType.DMA((parts, count)),
        ],
        compiler_params=pltpu.CompilerParams(collective_id=0, has_side_effects=True, vmem_limit_bytes=56 << 20),
    )(table)


def solution(mesh):
    in_specs = (
        P(None, ("parts", "xy"), None, None),
        P(None, ("parts", "xy"), None),
        P(("parts", "xy"), None, None),
        P(("parts", "xy"), None, None),
        P(("parts", "xy"), None),
        P("parts"),
    )
    out_specs = P(("parts", "xy"), None)
    return jax.shard_map(shards, mesh=mesh, in_specs=in_specs, out_specs=out_specs, check_vma=False)
```

```python
import functools
import math
import ml_dtypes
import numpy as np
import jax
import jax.numpy as jnp
from jax import lax
from jax.experimental import pallas as pl
from jax.experimental.pallas import tpu as pltpu
from jax.sharding import PartitionSpec as P

SLOTS = 8
HALO = 8
FEAT = 64
SIGMAS = (0.8, 1.3, 2.0, 3.0)
MESH = pl.DeviceIdType.MESH
VMEM = pltpu.VMEM


def taps(sigma):
    t = np.arange(-HALO, HALO + 1).astype(np.float64)
    w = np.exp(-t * t / (2.0 * sigma * sigma))
    return (w / w.sum()).astype(np.float32)


def band(sigma, length):
    w = taps(sigma)
    rows = np.arange(length)
    shift = rows[None, :] - rows[:, None] + HALO
    inside = (shift >= 0) & (shift <= 2 * HALO)
    full = np.where(inside, w[np.clip(shift, 0, 2 * HALO)], np.float32(0)).astype(np.float32)
    high = full.astype(ml_dtypes.bfloat16)
    low = (full - high.astype(np.float32)).astype(ml_dtypes.bfloat16)
    return high, low


def split(value):
    high = value.astype(jnp.bfloat16)
    low = (value - high.astype(jnp.float32)).astype(jnp.bfloat16)
    return high, low


def bits_of(n):
    return [1 << k for k in range(n.bit_length() - 1)]


def orders(n):
    bits = bits_of(n)
    late = bits[:1] + bits[2:] + bits[1:2]
    return (bits, late, bits, late)


def rank_of(dest, order):
    rank = jnp.zeros_like(dest)
    for bit in order:
        rank = rank * 2 + (dest // bit) % 2
    return rank


def blur_kernel(lists, affinity, scale, homes, along_y, along_z, out, own, place, ext, done_planes, send_sem, recv_sem, out_sem):
    planes, height, depth = affinity.shape[1:]
    n = lax.axis_size("xy")
    me = lax.axis_index("xy")
    part_id = lax.axis_index("parts")
    has_left, has_right = me > 0, me < n - 1
    left, right = (part_id, me - 1), (part_id, me + 1)
    barrier = pltpu.get_barrier_semaphore()

    for there, device in ((has_left, left), (has_right, right)):
        @pl.when(there)
        def _():
            pl.semaphore_signal(barrier, inc=1, device_id=device, device_id_type=MESH)
    for c in range(3):
        columns = jnp.transpose(scale[c], (1, 0))
        for p in range(planes):
            ext[c, HALO + p] = affinity[c, p].astype(jnp.float32) * columns[:, p:p + 1]

    inside = jnp.logical_and(has_left, has_right)

    @pl.when(inside)
    def _():
        pl.semaphore_wait(barrier, 2)

    @pl.when(jnp.logical_and(jnp.logical_not(inside), n > 1))
    def _():
        pl.semaphore_wait(barrier, 1)

    def to_right(p):
        return pltpu.make_async_remote_copy(
            src_ref=ext.at[:, HALO + p], dst_ref=ext.at[:, p],
            send_sem=send_sem.at[0, p], recv_sem=recv_sem.at[0, p],
            device_id=right, device_id_type=MESH)

    def to_left(p):
        return pltpu.make_async_remote_copy(
            src_ref=ext.at[:, HALO + p], dst_ref=ext.at[:, HALO + planes + p],
            send_sem=send_sem.at[1, p], recv_sem=recv_sem.at[1, p],
            device_id=left, device_id_type=MESH)

    side = me % 2
    even, odd = side == 0, side == 1

    def send_right(parity):
        @pl.when(jnp.logical_and(parity, has_right))
        def _():
            for p in reversed(range(planes)):
                to_right(p).start()

    def send_left(parity):
        @pl.when(jnp.logical_and(parity, has_left))
        def _():
            for p in range(planes):
                to_left(p).start()

    send_left(even)
    send_right(odd)
    send_right(even)
    send_left(odd)

    @pl.when(jnp.logical_not(has_left))
    def _():
        ext[:, :HALO] = jnp.zeros((3, HALO, height, depth), jnp.float32)

    @pl.when(jnp.logical_not(has_right))
    def _():
        ext[:, HALO + planes:] = jnp.zeros((3, HALO, height, depth), jnp.float32)

    own[...] = ext[:, HALO:HALO + planes]
    rows = homes.shape[0]
    e_dev = rows * 128 // n
    parts = len(lists)
    tile = e_dev // (2 * parts)
    home = homes[...]
    dest, inner = home // e_dev, home % e_dev
    half, inner = inner // (parts * tile), inner % (parts * tile)
    part, row = inner // tile, inner % tile
    rank = jnp.where(part % 2 == 1, rank_of(dest, lists[1]), rank_of(dest, lists[0]))
    place[:rows, :] = ((part * n + rank) * 2 + half) * tile + row
    place[rows:, :] = jnp.full((8, 128), rows * 128, jnp.int32)

    @pl.when(jnp.logical_and(even, has_right))
    def _():
        for p in range(planes):
            to_left(p).wait_recv()

    @pl.when(jnp.logical_and(odd, has_left))
    def _():
        for p in range(planes):
            to_right(p).wait_recv()

    weights = [taps(s) for s in SIGMAS]

    @pl.loop(0, planes)
    def _(step):
        @pl.when(jnp.logical_and(even, has_left))
        def _():
            to_right(planes - 1 - step).wait_recv()

        @pl.when(jnp.logical_and(odd, has_right))
        def _():
            to_left(step).wait_recv()

        q = step + (1 - side) * (planes - 1 - 2 * step)
        crossed = [[] for _ in SIGMAS]
        for c in range(3):
            chunks = [[] for _ in SIGMAS]
            for z in range(0, height, 16):
                mid = ext[c, q + HALO, z:z + 16, :]
                acc = [mid * float(w[HALO]) for w in weights]
                for t in range(1, HALO + 1):
                    both = ext[c, q + HALO - t, z:z + 16, :] + ext[c, q + HALO + t, z:z + 16, :]
                    acc = [a + both * float(w[HALO + t]) for a, w in zip(acc, weights)]
                for i in range(4):
                    chunks[i].append(acc[i])
            for i in range(4):
                crossed[i].append(jnp.concatenate(chunks[i], 0))
        for i in range(4):
            high, low = split(jnp.concatenate(crossed[i], 0))
            wide = jnp.dot(jnp.concatenate([high, low], 1), along_y[i], preferred_element_type=jnp.float32)
            field = wide[:, :depth] + wide[:, depth:]
            high, low = split(field)
            highs = jnp.concatenate([high[c * height:(c + 1) * height] for c in range(3)], 1)
            lows = jnp.concatenate([low[c * height:(c + 1) * height] for c in range(3)], 1)
            stacked = jnp.concatenate([highs, lows, highs, lows], 0)
            done = jnp.dot(along_z[i], stacked, preferred_element_type=jnp.float32)
            for c in range(3):
                done_planes[q, 3 * i + c] = done[:, c * depth:(c + 1) * depth]
        pltpu.make_async_copy(done_planes.at[q], out.at[q], out_sem.at[q]).start()

    for q in range(planes):
        pltpu.make_async_copy(done_planes.at[q], out.at[q], out_sem.at[q]).wait()

    @pl.when(has_right)
    def _():
        for p in range(planes):
            to_right(p).wait_send()

    @pl.when(has_left)
    def _():
        for p in range(planes):
            to_left(p).wait_send()


def sums_kernel(planes, banks, own, resp, slots, elist, place, out, rows, *tables):
    q = pl.program_id(0)
    height = own.shape[2]

    def add_rows(base):
        for e in range(128):
            at = place[elist[base + e]]
            table = tables[e % banks]
            table[pl.ds(at, 1), :] += rows[e:e + 1, :]

    @pl.when(q == 0)
    def _():
        rows[...] = jnp.zeros_like(rows)
        for table in tables:
            @pl.loop(0, table.shape[0] // 64)
            def _(r):
                table[pl.ds(pl.multiple_of(r * 64, 64), 64), :] = jnp.zeros((64, 128), jnp.float32)

    slot_row = lax.broadcasted_iota(jnp.int32, (SLOTS, 128), 0)
    lane = lax.broadcasted_iota(jnp.int32, (8, 128), 1)
    lane_z = (lane // SLOTS) % 8
    spread = (lax.broadcasted_iota(jnp.int32, (8, 128), 0) + 8 - lane_z) % 8

    @pl.loop(0, height // 16)
    def _(j):
        add_rows(jnp.maximum(q * (height * SLOTS) + j * 128 - 128, 0))
        z16 = pl.multiple_of(j * 16, 16)
        slot = slots[0, pl.ds(z16, 16), :]
        hot = jnp.concatenate([
            (jnp.broadcast_to(slot[k:k + 1, :], (SLOTS, 128)) == slot_row).astype(jnp.float32) for k in range(16)
        ], 0).astype(jnp.bfloat16)
        rhs = jnp.concatenate([hot, hot], 1)
        groups = []
        for g in range(2):
            z0 = pl.multiple_of(j * 16 + g * 8, 8)
            r = [resp[0, k, pl.ds(z0, 8), :] for k in range(12)]
            raw = [own[c, 0, pl.ds(z0, 8), :] for c in range(3)]
            square = [a * a for a in r]
            cube = [a * b for a, b in zip(square, r)]
            fourth = [a * a for a in square]
            pairs = []
            for i in range(4):
                a, b, c = r[3 * i:3 * i + 3]
                pairs += [a * b, a * c, b * c]
            ones = [jnp.ones((8, 128), jnp.float32)]
            groups.append(r + square + cube + fourth + pairs + raw + ones)
        pieces = []
        for f in range(0, FEAT, 8):
            feats = jnp.concatenate(groups[0][f:f + 8] + groups[1][f:f + 8], 0)
            high, low = split(feats)
            lhs = jnp.concatenate([high, low], 1)
            prod = lax.dot_general(lhs, rhs, (((1,), (1,)), ((), ())), preferred_element_type=jnp.float32)
            piece = None
            for k in range(8):
                both = jnp.where(lane < 64, prod[k * 8:k * 8 + 8], prod[64 + k * 8:64 + k * 8 + 8])
                piece = both if k == 0 else jnp.where(spread == k, pltpu.roll(both, k, 0), piece)
            for bit in (1, 2, 4):
                piece = jnp.where((lane_z // bit) % 2 == 1, pltpu.roll(piece, 8 - bit, 0), piece)
            pieces.append(piece)
        block = jnp.concatenate(pieces, 0)
        rows[...] = jnp.transpose(jnp.concatenate([block, jnp.zeros_like(block)], 0), (1, 0))

    @pl.when(q == pl.num_programs(0) - 1)
    def _():
        add_rows(planes * height * SLOTS - 128)
        tile = out.shape[2]
        low_lane = lax.broadcasted_iota(jnp.int32, (tile, 128), 1) < FEAT

        @pl.loop(0, out.shape[0] * out.shape[1])
        def _(b):
            def total(start):
                at = pl.ds(pl.multiple_of(start, 8), tile)
                value = tables[0][at, :]
                for table in tables[1:]:
                    value = value + table[at, :]
                return value
            first = total(b * 2 * tile)
            second = total(b * 2 * tile + tile)
            second = pltpu.roll(second, FEAT, 1)
            out[b // out.shape[1], b % out.shape[1]] = jnp.where(low_lane, first, second)


def reduce_kernel(n, lists, table, out, *scratch):
    count = n.bit_length() - 1
    recv = scratch[:count]
    acc = scratch[count:2 * count]
    send_sem, recv_sem = scratch[2 * count:]
    me = lax.axis_index("xy")
    part_id = lax.axis_index("parts")

    def partner(bit):
        return me + bit * (1 - 2 * ((me // bit) % 2))

    barrier = pltpu.get_barrier_semaphore()
    for bit in bits_of(n):
        pl.semaphore_signal(barrier, inc=1, device_id=(part_id, partner(bit)), device_id_type=MESH)
    pl.semaphore_wait(barrier, count)

    copies = {}
    lane = lax.broadcasted_iota(jnp.int32, table.shape[2:], 1)

    def start(p, k):
        bit = lists[p][k]
        size = n >> (k + 1)
        mine = (me // bit) % 2
        source = table.at[p] if k == 0 else acc[k - 1].at[p]
        copy = pltpu.make_async_remote_copy(
            src_ref=source.at[pl.ds((1 - mine) * size, size)],
            dst_ref=recv[k].at[p],
            send_sem=send_sem.at[p, k],
            recv_sem=recv_sem.at[p, k],
            device_id=(part_id, partner(bit)),
            device_id_type=MESH,
        )
        copy.start()
        copies[p, k] = copy

    def finish(p, k):
        bit = lists[p][k]
        size = n >> (k + 1)
        mine = (me // bit) % 2
        source = table.at[p] if k == 0 else acc[k - 1].at[p]
        copies[p, k].wait_recv()
        if k == count - 1:
            total = source[mine] + recv[k][p, 0]
            tile = total.shape[0]
            last = (lane % FEAT) == FEAT - 1
            low = jnp.where(lane < FEAT, total[:, FEAT - 1:FEAT], total[:, 2 * FEAT - 1:])
            done = jnp.where(last, jnp.log1p(total), total / jnp.maximum(low, 1.0))
            out[p * tile:(p + 1) * tile, :] = done[:, :FEAT]
            base = (len(lists) + p) * tile
            out[base:base + tile, :] = done[:, FEAT:]
        else:
            acc[k][p] = source[pl.ds(mine * size, size)] + recv[k][p]

    for p in range(len(lists)):
        start(p, 0)
    for k in range(count):
        for p in range(len(lists)):
            finish(p, k)
            if k + 1 < count:
                start(p, k + 1)
    for copy in copies.values():
        copy.wait_send()


def shards(affinity, block_scale, slot_map, edge_list, valid_count, edge_home):
    planes, height, depth = affinity.shape[1:]
    n = lax.axis_size("xy")
    edges = edge_home.shape[0]
    e_dev = edges // n
    lists = orders(n)
    parts = len(lists)
    tile = e_dev // (2 * parts)
    valid = jnp.arange(SLOTS, dtype=jnp.int32) < valid_count[..., None]
    elist = jnp.where(valid, edge_list, edges).reshape(-1)

    ys, zs = [], []
    for sigma in SIGMAS:
        high, low = band(sigma, depth)
        ys.append(np.block([[high, low], [high, low]]))
        high, low = band(sigma, height)
        zs.append(np.concatenate([high, high, low, low], 1))
    along_y = jnp.asarray(np.stack(ys), jnp.bfloat16)
    along_z = jnp.asarray(np.stack(zs), jnp.bfloat16)
    banks = 2 if edges * 512 * 4 <= (24 << 20) else 1
    whole = pl.BlockSpec(memory_space=VMEM)
    smem = pl.BlockSpec(memory_space=pltpu.SMEM)
    resp, dequant, place = pl.pallas_call(
        functools.partial(blur_kernel, lists),
        out_shape=[
            jax.ShapeDtypeStruct((planes, 12, height, depth), jnp.float32),
            jax.ShapeDtypeStruct((3, planes, height, depth), jnp.float32),
            jax.ShapeDtypeStruct((edges // 128 + 8, 128), jnp.int32),
        ],
        in_specs=[whole] * 5,
        out_specs=[pl.BlockSpec(memory_space=pl.ANY), whole, whole],
        scratch_shapes=[
            VMEM((3, planes + 2 * HALO, height, depth), jnp.float32),
            VMEM((planes, 12, height, depth), jnp.float32),
            pltpu.SemaphoreType.DMA((2, planes)),
            pltpu.SemaphoreType.DMA((2, planes)),
            pltpu.SemaphoreType.DMA((planes,)),
        ],
        compiler_params=pltpu.CompilerParams(collective_id=1, has_side_effects=True, vmem_limit_bytes=56 << 20),
    )(affinity, block_scale, edge_home.reshape(edges // 128, 128), along_y, along_z)
    table = pl.pallas_call(
        functools.partial(sums_kernel, planes, banks),
        grid=(planes,),
        out_shape=jax.ShapeDtypeStruct((parts, n, tile, 128), jnp.float32),
        in_specs=[
            pl.BlockSpec((3, 1, height, depth), lambda q: (0, q, 0, 0)),
            pl.BlockSpec((1, 12, height, depth), lambda q: (q, 0, 0, 0)),
            pl.BlockSpec((1, height, depth), lambda q: (q, 0, 0)),
            smem, smem,
        ],
        out_specs=whole,
        scratch_shapes=[
            VMEM((128, 128), jnp.float32),
        ] + [VMEM((edges + 64, 128), jnp.float32)] * banks,
        compiler_params=pltpu.CompilerParams(vmem_limit_bytes=56 << 20),
    )(dequant, resp, slot_map, elist, place.reshape(-1))

    count = n.bit_length() - 1
    sizes = [n >> (k + 1) for k in range(count)]
    return pl.pallas_call(
        functools.partial(reduce_kernel, n, lists),
        out_shape=jax.ShapeDtypeStruct((e_dev, FEAT), jnp.float32),
        in_specs=[whole],
        out_specs=whole,
        scratch_shapes=[VMEM((parts, s, tile, 128), jnp.float32) for s in sizes] * 2 + [
            pltpu.SemaphoreType.DMA((parts, count)),
            pltpu.SemaphoreType.DMA((parts, count)),
        ],
        compiler_params=pltpu.CompilerParams(collective_id=0, has_side_effects=True, vmem_limit_bytes=56 << 20),
    )(table)


def solution(mesh):
    in_specs = (
        P(None, ("parts", "xy"), None, None),
        P(None, ("parts", "xy"), None),
        P(("parts", "xy"), None, None),
        P(("parts", "xy"), None, None),
        P(("parts", "xy"), None),
        P("parts"),
    )
    out_specs = P(("parts", "xy"), None)
    return jax.shard_map(shards, mesh=mesh, in_specs=in_specs, out_specs=out_specs, check_vma=False)
```

```python
import functools
import math
import ml_dtypes
import numpy as np
import jax
import jax.numpy as jnp
from jax import lax
from jax.experimental import pallas as pl
from jax.experimental.pallas import tpu as pltpu
from jax.sharding import PartitionSpec as P

SLOTS = 8
HALO = 8
FEAT = 64
SIGMAS = (0.8, 1.3, 2.0, 3.0)
MESH = pl.DeviceIdType.MESH
VMEM = pltpu.VMEM


def taps(sigma):
    t = np.arange(-HALO, HALO + 1).astype(np.float64)
    w = np.exp(-t * t / (2.0 * sigma * sigma))
    return (w / w.sum()).astype(np.float32)


def band(sigma, length):
    w = taps(sigma)
    rows = np.arange(length)
    shift = rows[None, :] - rows[:, None] + HALO
    inside = (shift >= 0) & (shift <= 2 * HALO)
    full = np.where(inside, w[np.clip(shift, 0, 2 * HALO)], np.float32(0)).astype(np.float32)
    high = full.astype(ml_dtypes.bfloat16)
    low = (full - high.astype(np.float32)).astype(ml_dtypes.bfloat16)
    return high, low


def split(value):
    high = value.astype(jnp.bfloat16)
    low = (value - high.astype(jnp.float32)).astype(jnp.bfloat16)
    return high, low


def bits_of(n):
    return [1 << k for k in range(n.bit_length() - 1)]


def orders(n):
    bits = bits_of(n)
    late = bits[:1] + bits[2:] + bits[1:2]
    return (bits, late, bits, late)


def rank_of(dest, order):
    rank = jnp.zeros_like(dest)
    for bit in order:
        rank = rank * 2 + (dest // bit) % 2
    return rank


def blur_kernel(lists, affinity, scale, homes, along_y, along_z, out, own, place, ext, done_planes, send_sem, recv_sem, out_sem):
    planes, height, depth = affinity.shape[1:]
    n = lax.axis_size("xy")
    me = lax.axis_index("xy")
    part_id = lax.axis_index("parts")
    has_left, has_right = me > 0, me < n - 1
    left, right = (part_id, me - 1), (part_id, me + 1)
    barrier = pltpu.get_barrier_semaphore()

    for there, device in ((has_left, left), (has_right, right)):
        @pl.when(there)
        def _():
            pl.semaphore_signal(barrier, inc=1, device_id=device, device_id_type=MESH)
    for c in range(3):
        columns = jnp.transpose(scale[c], (1, 0))
        for p in range(planes):
            ext[c, HALO + p] = affinity[c, p].astype(jnp.float32) * columns[:, p:p + 1]

    inside = jnp.logical_and(has_left, has_right)

    @pl.when(inside)
    def _():
        pl.semaphore_wait(barrier, 2)

    @pl.when(jnp.logical_and(jnp.logical_not(inside), n > 1))
    def _():
        pl.semaphore_wait(barrier, 1)

    def to_right(p):
        return pltpu.make_async_remote_copy(
            src_ref=ext.at[:, HALO + p], dst_ref=ext.at[:, p],
            send_sem=send_sem.at[0, p], recv_sem=recv_sem.at[0, p],
            device_id=right, device_id_type=MESH)

    def to_left(p):
        return pltpu.make_async_remote_copy(
            src_ref=ext.at[:, HALO + p], dst_ref=ext.at[:, HALO + planes + p],
            send_sem=send_sem.at[1, p], recv_sem=recv_sem.at[1, p],
            device_id=left, device_id_type=MESH)

    side = me % 2
    even, odd = side == 0, side == 1

    def send_right(parity):
        @pl.when(jnp.logical_and(parity, has_right))
        def _():
            for p in reversed(range(planes)):
                to_right(p).start()

    def send_left(parity):
        @pl.when(jnp.logical_and(parity, has_left))
        def _():
            for p in range(planes):
                to_left(p).start()

    send_left(even)
    send_right(odd)
    send_right(even)
    send_left(odd)

    @pl.when(jnp.logical_not(has_left))
    def _():
        ext[:, :HALO] = jnp.zeros((3, HALO, height, depth), jnp.float32)

    @pl.when(jnp.logical_not(has_right))
    def _():
        ext[:, HALO + planes:] = jnp.zeros((3, HALO, height, depth), jnp.float32)

    own[...] = ext[:, HALO:HALO + planes]
    rows = homes.shape[0]
    e_dev = rows * 128 // n
    parts = len(lists)
    tile = e_dev // (2 * parts)
    home = homes[...]
    dest, inner = home // e_dev, home % e_dev
    half, inner = inner // (parts * tile), inner % (parts * tile)
    part, row = inner // tile, inner % tile
    rank = jnp.where(part % 2 == 1, rank_of(dest, lists[1]), rank_of(dest, lists[0]))
    place[:rows, :] = ((part * n + rank) * 2 + half) * tile + row
    place[rows:, :] = jnp.full((8, 128), rows * 128, jnp.int32)

    @pl.when(jnp.logical_and(even, has_right))
    def _():
        for p in range(planes):
            to_left(p).wait_recv()

    @pl.when(jnp.logical_and(odd, has_left))
    def _():
        for p in range(planes):
            to_right(p).wait_recv()

    weights = [taps(s) for s in SIGMAS]

    @pl.loop(0, planes)
    def _(step):
        @pl.when(jnp.logical_and(even, has_left))
        def _():
            to_right(planes - 1 - step).wait_recv()

        @pl.when(jnp.logical_and(odd, has_right))
        def _():
            to_left(step).wait_recv()

        q = step + (1 - side) * (planes - 1 - 2 * step)
        crossed = [[] for _ in SIGMAS]
        for c in range(3):
            chunks = [[] for _ in SIGMAS]
            for z in range(0, height, 16):
                mid = ext[c, q + HALO, z:z + 16, :]
                acc = [mid * float(w[HALO]) for w in weights]
                for t in range(1, HALO + 1):
                    both = ext[c, q + HALO - t, z:z + 16, :] + ext[c, q + HALO + t, z:z + 16, :]
                    acc = [a + both * float(w[HALO + t]) for a, w in zip(acc, weights)]
                for i in range(4):
                    chunks[i].append(acc[i])
            for i in range(4):
                crossed[i].append(jnp.concatenate(chunks[i], 0))
        for i in range(4):
            high, low = split(jnp.concatenate(crossed[i], 0))
            wide = jnp.dot(jnp.concatenate([high, low], 1), along_y[i], preferred_element_type=jnp.float32)
            field = wide[:, :depth] + wide[:, depth:]
            high, low = split(field)
            highs = jnp.concatenate([high[c * height:(c + 1) * height] for c in range(3)], 1)
            lows = jnp.concatenate([low[c * height:(c + 1) * height] for c in range(3)], 1)
            stacked = jnp.concatenate([highs, lows, highs, lows], 0)
            done = jnp.dot(along_z[i], stacked, preferred_element_type=jnp.float32)
            for c in range(3):
                done_planes[q, 3 * i + c] = done[:, c * depth:(c + 1) * depth]
        pltpu.make_async_copy(done_planes.at[q], out.at[q], out_sem.at[q]).start()

    for q in range(planes):
        pltpu.make_async_copy(done_planes.at[q], out.at[q], out_sem.at[q]).wait()

    @pl.when(has_right)
    def _():
        for p in range(planes):
            to_right(p).wait_send()

    @pl.when(has_left)
    def _():
        for p in range(planes):
            to_left(p).wait_send()


def sums_kernel(planes, banks, own, resp, slots, elist, place, out, rows, *tables):
    q = pl.program_id(0)
    height = own.shape[2]

    def add_rows(base):
        for e in range(128):
            at = place[elist[base + e]]
            table = tables[e % banks]
            table[pl.ds(at, 1), :] += rows[e:e + 1, :]

    @pl.when(q == 0)
    def _():
        rows[...] = jnp.zeros_like(rows)
        for table in tables:
            @pl.loop(0, table.shape[0] // 64)
            def _(r):
                table[pl.ds(pl.multiple_of(r * 64, 64), 64), :] = jnp.zeros((64, 128), jnp.float32)

    slot_row = lax.broadcasted_iota(jnp.int32, (SLOTS, 128), 0)
    lane = lax.broadcasted_iota(jnp.int32, (8, 128), 1)
    lane_z = (lane // SLOTS) % 8
    spread = (lax.broadcasted_iota(jnp.int32, (8, 128), 0) + 8 - lane_z) % 8

    @pl.loop(0, height // 16)
    def _(j):
        add_rows(jnp.maximum(q * (height * SLOTS) + j * 128 - 128, 0))
        z16 = pl.multiple_of(j * 16, 16)
        slot = slots[0, pl.ds(z16, 16), :]
        hot = jnp.concatenate([
            (jnp.broadcast_to(slot[k:k + 1, :], (SLOTS, 128)) == slot_row).astype(jnp.float32) for k in range(16)
        ], 0).astype(jnp.bfloat16)
        rhs = jnp.concatenate([hot, hot], 1)
        groups = []
        for g in range(2):
            z0 = pl.multiple_of(j * 16 + g * 8, 8)
            r = [resp[0, k, pl.ds(z0, 8), :] for k in range(12)]
            raw = [own[c, 0, pl.ds(z0, 8), :] for c in range(3)]
            square = [a * a for a in r]
            cube = [a * b for a, b in zip(square, r)]
            fourth = [a * a for a in square]
            pairs = []
            for i in range(4):
                a, b, c = r[3 * i:3 * i + 3]
                pairs += [a * b, a * c, b * c]
            ones = [jnp.ones((8, 128), jnp.float32)]
            groups.append(r + square + cube + fourth + pairs + raw + ones)
        pieces = []
        for f in range(0, FEAT, 8):
            feats = jnp.concatenate(groups[0][f:f + 8] + groups[1][f:f + 8], 0)
            high, low = split(feats)
            lhs = jnp.concatenate([high, low], 1)
            prod = lax.dot_general(lhs, rhs, (((1,), (1,)), ((), ())), preferred_element_type=jnp.float32)
            piece = None
            for k in range(8):
                both = jnp.where(lane < 64, prod[k * 8:k * 8 + 8], prod[64 + k * 8:64 + k * 8 + 8])
                piece = both if k == 0 else jnp.where(spread == k, pltpu.roll(both, k, 0), piece)
            for bit in (1, 2, 4):
                piece = jnp.where((lane_z // bit) % 2 == 1, pltpu.roll(piece, 8 - bit, 0), piece)
            pieces.append(piece)
        block = jnp.concatenate(pieces, 0)
        rows[...] = jnp.transpose(jnp.concatenate([block, jnp.zeros_like(block)], 0), (1, 0))

    @pl.when(q == pl.num_programs(0) - 1)
    def _():
        add_rows(planes * height * SLOTS - 128)
        tile = out.shape[2]
        low_lane = lax.broadcasted_iota(jnp.int32, (tile, 128), 1) < FEAT

        @pl.loop(0, out.shape[0] * out.shape[1])
        def _(b):
            def total(start):
                at = pl.ds(pl.multiple_of(start, 8), tile)
                value = tables[0][at, :]
                for table in tables[1:]:
                    value = value + table[at, :]
                return value
            first = total(b * 2 * tile)
            second = total(b * 2 * tile + tile)
            second = pltpu.roll(second, FEAT, 1)
            out[b // out.shape[1], b % out.shape[1]] = jnp.where(low_lane, first, second)


def reduce_kernel(n, lists, table, out, *scratch):
    count = n.bit_length() - 1
    recv = scratch[:count]
    acc = scratch[count:2 * count]
    kept, send_sem, recv_sem, keep_sem = scratch[2 * count:]
    me = lax.axis_index("xy")
    part_id = lax.axis_index("parts")

    def partner(bit):
        return me + bit * (1 - 2 * ((me // bit) % 2))

    barrier = pltpu.get_barrier_semaphore()
    for bit in bits_of(n):
        pl.semaphore_signal(barrier, inc=1, device_id=(part_id, partner(bit)), device_id_type=MESH)
    pl.semaphore_wait(barrier, count)

    copies = {}
    lane = lax.broadcasted_iota(jnp.int32, table.shape[2:], 1)

    def keep(p):
        mine = (me // lists[p][0]) % 2
        return pltpu.make_async_copy(table.at[p, pl.ds(mine * (n // 2), n // 2)], kept.at[p], keep_sem.at[p])

    def start(p, k):
        bit = lists[p][k]
        size = n >> (k + 1)
        mine = (me // bit) % 2
        source = table.at[p] if k == 0 else acc[k - 1].at[p]
        copy = pltpu.make_async_remote_copy(
            src_ref=source.at[pl.ds((1 - mine) * size, size)],
            dst_ref=recv[k].at[p],
            send_sem=send_sem.at[p, k],
            recv_sem=recv_sem.at[p, k],
            device_id=(part_id, partner(bit)),
            device_id_type=MESH,
        )
        copy.start()
        copies[p, k] = copy

    def finish(p, k):
        bit = lists[p][k]
        size = n >> (k + 1)
        mine = (me // bit) % 2
        source = table.at[p] if k == 0 else acc[k - 1].at[p]
        copies[p, k].wait_recv()
        if k == 0:
            keep(p).wait()
            mine_now = kept[p]
        else:
            mine_now = source[mine] if size == 1 else source[pl.ds(mine * size, size)]
        if k == count - 1:
            total = mine_now.reshape(recv[k].shape[2:]) + recv[k][p, 0]
            tile = total.shape[0]
            last = (lane % FEAT) == FEAT - 1
            low = jnp.where(lane < FEAT, total[:, FEAT - 1:FEAT], total[:, 2 * FEAT - 1:])
            done = jnp.where(last, jnp.log1p(total), total / jnp.maximum(low, 1.0))
            out[p * tile:(p + 1) * tile, :] = done[:, :FEAT]
            base = (len(lists) + p) * tile
            out[base:base + tile, :] = done[:, FEAT:]
        else:
            acc[k][p] = mine_now.reshape(recv[k].shape[1:]) + recv[k][p]

    for p in range(len(lists)):
        start(p, 0)
    for p in range(len(lists)):
        keep(p).start()
    for k in range(count):
        for p in range(len(lists)):
            finish(p, k)
            if k + 1 < count:
                start(p, k + 1)
    for copy in copies.values():
        copy.wait_send()


def shards(affinity, block_scale, slot_map, edge_list, valid_count, edge_home):
    planes, height, depth = affinity.shape[1:]
    n = lax.axis_size("xy")
    edges = edge_home.shape[0]
    e_dev = edges // n
    lists = orders(n)
    parts = len(lists)
    tile = e_dev // (2 * parts)
    valid = jnp.arange(SLOTS, dtype=jnp.int32) < valid_count[..., None]
    elist = jnp.where(valid, edge_list, edges).reshape(-1)

    ys, zs = [], []
    for sigma in SIGMAS:
        high, low = band(sigma, depth)
        ys.append(np.block([[high, low], [high, low]]))
        high, low = band(sigma, height)
        zs.append(np.concatenate([high, high, low, low], 1))
    along_y = jnp.asarray(np.stack(ys), jnp.bfloat16)
    along_z = jnp.asarray(np.stack(zs), jnp.bfloat16)
    banks = 2 if edges * 512 * 4 <= (24 << 20) else 1
    whole = pl.BlockSpec(memory_space=VMEM)
    smem = pl.BlockSpec(memory_space=pltpu.SMEM)
    resp, dequant, place = pl.pallas_call(
        functools.partial(blur_kernel, lists),
        out_shape=[
            jax.ShapeDtypeStruct((planes, 12, height, depth), jnp.float32),
            jax.ShapeDtypeStruct((3, planes, height, depth), jnp.float32),
            jax.ShapeDtypeStruct((edges // 128 + 8, 128), jnp.int32),
        ],
        in_specs=[whole] * 5,
        out_specs=[pl.BlockSpec(memory_space=pl.ANY), whole, whole],
        scratch_shapes=[
            VMEM((3, planes + 2 * HALO, height, depth), jnp.float32),
            VMEM((planes, 12, height, depth), jnp.float32),
            pltpu.SemaphoreType.DMA((2, planes)),
            pltpu.SemaphoreType.DMA((2, planes)),
            pltpu.SemaphoreType.DMA((planes,)),
        ],
        compiler_params=pltpu.CompilerParams(collective_id=1, has_side_effects=True, vmem_limit_bytes=56 << 20),
    )(affinity, block_scale, edge_home.reshape(edges // 128, 128), along_y, along_z)
    table = pl.pallas_call(
        functools.partial(sums_kernel, planes, banks),
        grid=(planes,),
        out_shape=jax.ShapeDtypeStruct((parts, n, tile, 128), jnp.float32),
        in_specs=[
            pl.BlockSpec((3, 1, height, depth), lambda q: (0, q, 0, 0)),
            pl.BlockSpec((1, 12, height, depth), lambda q: (q, 0, 0, 0)),
            pl.BlockSpec((1, height, depth), lambda q: (q, 0, 0)),
            smem, smem,
        ],
        out_specs=whole,
        scratch_shapes=[
            VMEM((128, 128), jnp.float32),
        ] + [VMEM((edges + 64, 128), jnp.float32)] * banks,
        compiler_params=pltpu.CompilerParams(vmem_limit_bytes=56 << 20),
    )(dequant, resp, slot_map, elist, place.reshape(-1))

    count = n.bit_length() - 1
    sizes = [n >> (k + 1) for k in range(count)]
    return pl.pallas_call(
        functools.partial(reduce_kernel, n, lists),
        out_shape=jax.ShapeDtypeStruct((e_dev, FEAT), jnp.float32),
        in_specs=[pl.BlockSpec(memory_space=pl.ANY)],
        out_specs=whole,
        scratch_shapes=[VMEM((parts, s, tile, 128), jnp.float32) for s in sizes] * 2 + [
            VMEM((parts, n // 2, tile, 128), jnp.float32),
            pltpu.SemaphoreType.DMA((parts, count)),
            pltpu.SemaphoreType.DMA((parts, count)),
            pltpu.SemaphoreType.DMA((parts,)),
        ],
        compiler_params=pltpu.CompilerParams(collective_id=0, has_side_effects=True, vmem_limit_bytes=56 << 20),
    )(table)


def solution(mesh):
    in_specs = (
        P(None, ("parts", "xy"), None, None),
        P(None, ("parts", "xy"), None),
        P(("parts", "xy"), None, None),
        P(("parts", "xy"), None, None),
        P(("parts", "xy"), None),
        P("parts"),
    )
    out_specs = P(("parts", "xy"), None)
    return jax.shard_map(shards, mesh=mesh, in_specs=in_specs, out_specs=out_specs, check_vma=False)
```

```python
import functools
import math
import ml_dtypes
import numpy as np
import jax
import jax.numpy as jnp
from jax import lax
from jax.experimental import pallas as pl
from jax.experimental.pallas import tpu as pltpu
from jax.sharding import PartitionSpec as P

SLOTS = 8
HALO = 8
FEAT = 64
SIGMAS = (0.8, 1.3, 2.0, 3.0)
MESH = pl.DeviceIdType.MESH
VMEM = pltpu.VMEM


def taps(sigma):
    t = np.arange(-HALO, HALO + 1).astype(np.float64)
    w = np.exp(-t * t / (2.0 * sigma * sigma))
    return (w / w.sum()).astype(np.float32)


def band(sigma, length):
    w = taps(sigma)
    rows = np.arange(length)
    shift = rows[None, :] - rows[:, None] + HALO
    inside = (shift >= 0) & (shift <= 2 * HALO)
    full = np.where(inside, w[np.clip(shift, 0, 2 * HALO)], np.float32(0)).astype(np.float32)
    high = full.astype(ml_dtypes.bfloat16)
    low = (full - high.astype(np.float32)).astype(ml_dtypes.bfloat16)
    return high, low


def split(value):
    high = value.astype(jnp.bfloat16)
    low = (value - high.astype(jnp.float32)).astype(jnp.bfloat16)
    return high, low


def bits_of(n):
    return [1 << k for k in range(n.bit_length() - 1)]


def orders(n):
    bits = bits_of(n)
    late = bits[:1] + bits[2:] + bits[1:2]
    return (bits, late) * 4


def rank_of(dest, order):
    rank = jnp.zeros_like(dest)
    for bit in order:
        rank = rank * 2 + (dest // bit) % 2
    return rank


def blur_kernel(lists, affinity, scale, homes, along_y, along_z, out, own, place, ext, done_planes, send_sem, recv_sem, out_sem):
    planes, height, depth = affinity.shape[1:]
    n = lax.axis_size("xy")
    me = lax.axis_index("xy")
    part_id = lax.axis_index("parts")
    has_left, has_right = me > 0, me < n - 1
    left, right = (part_id, me - 1), (part_id, me + 1)
    barrier = pltpu.get_barrier_semaphore()

    for there, device in ((has_left, left), (has_right, right)):
        @pl.when(there)
        def _():
            pl.semaphore_signal(barrier, inc=1, device_id=device, device_id_type=MESH)
    for c in range(3):
        columns = jnp.transpose(scale[c], (1, 0))
        for p in range(planes):
            ext[c, HALO + p] = affinity[c, p].astype(jnp.float32) * columns[:, p:p + 1]

    inside = jnp.logical_and(has_left, has_right)

    @pl.when(inside)
    def _():
        pl.semaphore_wait(barrier, 2)

    @pl.when(jnp.logical_and(jnp.logical_not(inside), n > 1))
    def _():
        pl.semaphore_wait(barrier, 1)

    def to_right(p):
        return pltpu.make_async_remote_copy(
            src_ref=ext.at[:, HALO + p], dst_ref=ext.at[:, p],
            send_sem=send_sem.at[0, p], recv_sem=recv_sem.at[0, p],
            device_id=right, device_id_type=MESH)

    def to_left(p):
        return pltpu.make_async_remote_copy(
            src_ref=ext.at[:, HALO + p], dst_ref=ext.at[:, HALO + planes + p],
            send_sem=send_sem.at[1, p], recv_sem=recv_sem.at[1, p],
            device_id=left, device_id_type=MESH)

    side = me % 2
    even, odd = side == 0, side == 1

    def send_right(parity):
        @pl.when(jnp.logical_and(parity, has_right))
        def _():
            for p in reversed(range(planes)):
                to_right(p).start()

    def send_left(parity):
        @pl.when(jnp.logical_and(parity, has_left))
        def _():
            for p in range(planes):
                to_left(p).start()

    send_left(even)
    send_right(odd)
    send_right(even)
    send_left(odd)

    @pl.when(jnp.logical_not(has_left))
    def _():
        ext[:, :HALO] = jnp.zeros((3, HALO, height, depth), jnp.float32)

    @pl.when(jnp.logical_not(has_right))
    def _():
        ext[:, HALO + planes:] = jnp.zeros((3, HALO, height, depth), jnp.float32)

    own[...] = ext[:, HALO:HALO + planes]
    rows = homes.shape[0]
    e_dev = rows * 128 // n
    parts = len(lists)
    tile = e_dev // (2 * parts)
    home = homes[...]
    dest, inner = home // e_dev, home % e_dev
    half, inner = inner // (parts * tile), inner % (parts * tile)
    part, row = inner // tile, inner % tile
    rank = jnp.where(part % 2 == 1, rank_of(dest, lists[1]), rank_of(dest, lists[0]))
    place[:rows, :] = ((part * n + rank) * 2 + half) * tile + row
    place[rows:, :] = jnp.full((8, 128), rows * 128, jnp.int32)

    @pl.when(jnp.logical_and(even, has_right))
    def _():
        for p in range(planes):
            to_left(p).wait_recv()

    @pl.when(jnp.logical_and(odd, has_left))
    def _():
        for p in range(planes):
            to_right(p).wait_recv()

    weights = [taps(s) for s in SIGMAS]

    @pl.loop(0, planes)
    def _(step):
        @pl.when(jnp.logical_and(even, has_left))
        def _():
            to_right(planes - 1 - step).wait_recv()

        @pl.when(jnp.logical_and(odd, has_right))
        def _():
            to_left(step).wait_recv()

        q = step + (1 - side) * (planes - 1 - 2 * step)
        crossed = [[] for _ in SIGMAS]
        for c in range(3):
            chunks = [[] for _ in SIGMAS]
            for z in range(0, height, 16):
                mid = ext[c, q + HALO, z:z + 16, :]
                acc = [mid * float(w[HALO]) for w in weights]
                for t in range(1, HALO + 1):
                    both = ext[c, q + HALO - t, z:z + 16, :] + ext[c, q + HALO + t, z:z + 16, :]
                    acc = [a + both * float(w[HALO + t]) for a, w in zip(acc, weights)]
                for i in range(4):
                    chunks[i].append(acc[i])
            for i in range(4):
                crossed[i].append(jnp.concatenate(chunks[i], 0))
        for i in range(4):
            high, low = split(jnp.concatenate(crossed[i], 0))
            wide = jnp.dot(jnp.concatenate([high, low], 1), along_y[i], preferred_element_type=jnp.float32)
            field = wide[:, :depth] + wide[:, depth:]
            high, low = split(field)
            highs = jnp.concatenate([high[c * height:(c + 1) * height] for c in range(3)], 1)
            lows = jnp.concatenate([low[c * height:(c + 1) * height] for c in range(3)], 1)
            stacked = jnp.concatenate([highs, lows, highs, lows], 0)
            done = jnp.dot(along_z[i], stacked, preferred_element_type=jnp.float32)
            for c in range(3):
                done_planes[q, 3 * i + c] = done[:, c * depth:(c + 1) * depth]
        pltpu.make_async_copy(done_planes.at[q], out.at[q], out_sem.at[q]).start()

    for q in range(planes):
        pltpu.make_async_copy(done_planes.at[q], out.at[q], out_sem.at[q]).wait()

    @pl.when(has_right)
    def _():
        for p in range(planes):
            to_right(p).wait_send()

    @pl.when(has_left)
    def _():
        for p in range(planes):
            to_left(p).wait_send()


def sums_kernel(planes, banks, own, resp, slots, elist, place, out, rows, *tables):
    q = pl.program_id(0)
    height = own.shape[2]

    def add_rows(base):
        for e in range(128):
            at = place[elist[base + e]]
            table = tables[e % banks]
            table[pl.ds(at, 1), :] += rows[e:e + 1, :]

    @pl.when(q == 0)
    def _():
        rows[...] = jnp.zeros_like(rows)
        for table in tables:
            @pl.loop(0, table.shape[0] // 64)
            def _(r):
                table[pl.ds(pl.multiple_of(r * 64, 64), 64), :] = jnp.zeros((64, 128), jnp.float32)

    slot_row = lax.broadcasted_iota(jnp.int32, (SLOTS, 128), 0)
    lane = lax.broadcasted_iota(jnp.int32, (8, 128), 1)
    lane_z = (lane // SLOTS) % 8
    spread = (lax.broadcasted_iota(jnp.int32, (8, 128), 0) + 8 - lane_z) % 8

    @pl.loop(0, height // 16)
    def _(j):
        add_rows(jnp.maximum(q * (height * SLOTS) + j * 128 - 128, 0))
        z16 = pl.multiple_of(j * 16, 16)
        slot = slots[0, pl.ds(z16, 16), :]
        hot = jnp.concatenate([
            (jnp.broadcast_to(slot[k:k + 1, :], (SLOTS, 128)) == slot_row).astype(jnp.float32) for k in range(16)
        ], 0).astype(jnp.bfloat16)
        rhs = jnp.concatenate([hot, hot], 1)
        groups = []
        for g in range(2):
            z0 = pl.multiple_of(j * 16 + g * 8, 8)
            r = [resp[0, k, pl.ds(z0, 8), :] for k in range(12)]
            raw = [own[c, 0, pl.ds(z0, 8), :] for c in range(3)]
            square = [a * a for a in r]
            cube = [a * b for a, b in zip(square, r)]
            fourth = [a * a for a in square]
            pairs = []
            for i in range(4):
                a, b, c = r[3 * i:3 * i + 3]
                pairs += [a * b, a * c, b * c]
            ones = [jnp.ones((8, 128), jnp.float32)]
            groups.append(r + square + cube + fourth + pairs + raw + ones)
        pieces = []
        for f in range(0, FEAT, 8):
            feats = jnp.concatenate(groups[0][f:f + 8] + groups[1][f:f + 8], 0)
            high, low = split(feats)
            lhs = jnp.concatenate([high, low], 1)
            prod = lax.dot_general(lhs, rhs, (((1,), (1,)), ((), ())), preferred_element_type=jnp.float32)
            piece = None
            for k in range(8):
                both = jnp.where(lane < 64, prod[k * 8:k * 8 + 8], prod[64 + k * 8:64 + k * 8 + 8])
                piece = both if k == 0 else jnp.where(spread == k, pltpu.roll(both, k, 0), piece)
            for bit in (1, 2, 4):
                piece = jnp.where((lane_z // bit) % 2 == 1, pltpu.roll(piece, 8 - bit, 0), piece)
            pieces.append(piece)
        block = jnp.concatenate(pieces, 0)
        rows[...] = jnp.transpose(jnp.concatenate([block, jnp.zeros_like(block)], 0), (1, 0))

    @pl.when(q == pl.num_programs(0) - 1)
    def _():
        add_rows(planes * height * SLOTS - 128)
        tile = out.shape[2]
        low_lane = lax.broadcasted_iota(jnp.int32, (tile, 128), 1) < FEAT

        @pl.loop(0, out.shape[0] * out.shape[1])
        def _(b):
            def total(start):
                at = pl.ds(pl.multiple_of(start, 8), tile)
                value = tables[0][at, :]
                for table in tables[1:]:
                    value = value + table[at, :]
                return value
            first = total(b * 2 * tile)
            second = total(b * 2 * tile + tile)
            second = pltpu.roll(second, FEAT, 1)
            out[b // out.shape[1], b % out.shape[1]] = jnp.where(low_lane, first, second)


def reduce_kernel(n, lists, table, out, *scratch):
    count = n.bit_length() - 1
    recv = scratch[:count]
    acc = scratch[count:2 * count]
    kept, send_sem, recv_sem, keep_sem = scratch[2 * count:]
    me = lax.axis_index("xy")
    part_id = lax.axis_index("parts")

    def partner(bit):
        return me + bit * (1 - 2 * ((me // bit) % 2))

    barrier = pltpu.get_barrier_semaphore()
    for bit in bits_of(n):
        pl.semaphore_signal(barrier, inc=1, device_id=(part_id, partner(bit)), device_id_type=MESH)
    pl.semaphore_wait(barrier, count)

    copies = {}
    lane = lax.broadcasted_iota(jnp.int32, table.shape[2:], 1)

    def keep(p):
        mine = (me // lists[p][0]) % 2
        return pltpu.make_async_copy(table.at[p, pl.ds(mine * (n // 2), n // 2)], kept.at[p], keep_sem.at[p])

    def start(p, k):
        bit = lists[p][k]
        size = n >> (k + 1)
        mine = (me // bit) % 2
        source = table.at[p] if k == 0 else acc[k - 1].at[p]
        copy = pltpu.make_async_remote_copy(
            src_ref=source.at[pl.ds((1 - mine) * size, size)],
            dst_ref=recv[k].at[p],
            send_sem=send_sem.at[p, k],
            recv_sem=recv_sem.at[p, k],
            device_id=(part_id, partner(bit)),
            device_id_type=MESH,
        )
        copy.start()
        copies[p, k] = copy

    def finish(p, k):
        bit = lists[p][k]
        size = n >> (k + 1)
        mine = (me // bit) % 2
        source = table.at[p] if k == 0 else acc[k - 1].at[p]
        copies[p, k].wait_recv()
        if k == 0:
            keep(p).wait()
            mine_now = kept[p]
        else:
            mine_now = source[mine] if size == 1 else source[pl.ds(mine * size, size)]
        if k == count - 1:
            total = mine_now.reshape(recv[k].shape[2:]) + recv[k][p, 0]
            tile = total.shape[0]
            last = (lane % FEAT) == FEAT - 1
            low = jnp.where(lane < FEAT, total[:, FEAT - 1:FEAT], total[:, 2 * FEAT - 1:])
            done = jnp.where(last, jnp.log1p(total), total / jnp.maximum(low, 1.0))
            out[p * tile:(p + 1) * tile, :] = done[:, :FEAT]
            base = (len(lists) + p) * tile
            out[base:base + tile, :] = done[:, FEAT:]
        else:
            acc[k][p] = mine_now.reshape(recv[k].shape[1:]) + recv[k][p]

    for p in range(len(lists)):
        start(p, 0)
    for p in range(len(lists)):
        keep(p).start()
    for k in range(count):
        for p in range(len(lists)):
            finish(p, k)
            if k + 1 < count:
                start(p, k + 1)
    for copy in copies.values():
        copy.wait_send()


def shards(affinity, block_scale, slot_map, edge_list, valid_count, edge_home):
    planes, height, depth = affinity.shape[1:]
    n = lax.axis_size("xy")
    edges = edge_home.shape[0]
    e_dev = edges // n
    lists = orders(n)
    parts = len(lists)
    tile = e_dev // (2 * parts)
    valid = jnp.arange(SLOTS, dtype=jnp.int32) < valid_count[..., None]
    elist = jnp.where(valid, edge_list, edges).reshape(-1)

    ys, zs = [], []
    for sigma in SIGMAS:
        high, low = band(sigma, depth)
        ys.append(np.block([[high, low], [high, low]]))
        high, low = band(sigma, height)
        zs.append(np.concatenate([high, high, low, low], 1))
    along_y = jnp.asarray(np.stack(ys), jnp.bfloat16)
    along_z = jnp.asarray(np.stack(zs), jnp.bfloat16)
    banks = 2 if edges * 512 * 4 <= (24 << 20) else 1
    whole = pl.BlockSpec(memory_space=VMEM)
    smem = pl.BlockSpec(memory_space=pltpu.SMEM)
    resp, dequant, place = pl.pallas_call(
        functools.partial(blur_kernel, lists),
        out_shape=[
            jax.ShapeDtypeStruct((planes, 12, height, depth), jnp.float32),
            jax.ShapeDtypeStruct((3, planes, height, depth), jnp.float32),
            jax.ShapeDtypeStruct((edges // 128 + 8, 128), jnp.int32),
        ],
        in_specs=[whole] * 5,
        out_specs=[pl.BlockSpec(memory_space=pl.ANY), whole, whole],
        scratch_shapes=[
            VMEM((3, planes + 2 * HALO, height, depth), jnp.float32),
            VMEM((planes, 12, height, depth), jnp.float32),
            pltpu.SemaphoreType.DMA((2, planes)),
            pltpu.SemaphoreType.DMA((2, planes)),
            pltpu.SemaphoreType.DMA((planes,)),
        ],
        compiler_params=pltpu.CompilerParams(collective_id=1, has_side_effects=True, vmem_limit_bytes=56 << 20),
    )(affinity, block_scale, edge_home.reshape(edges // 128, 128), along_y, along_z)
    table = pl.pallas_call(
        functools.partial(sums_kernel, planes, banks),
        grid=(planes,),
        out_shape=jax.ShapeDtypeStruct((parts, n, tile, 128), jnp.float32),
        in_specs=[
            pl.BlockSpec((3, 1, height, depth), lambda q: (0, q, 0, 0)),
            pl.BlockSpec((1, 12, height, depth), lambda q: (q, 0, 0, 0)),
            pl.BlockSpec((1, height, depth), lambda q: (q, 0, 0)),
            smem, smem,
        ],
        out_specs=whole,
        scratch_shapes=[
            VMEM((128, 128), jnp.float32),
        ] + [VMEM((edges + 64, 128), jnp.float32)] * banks,
        compiler_params=pltpu.CompilerParams(vmem_limit_bytes=56 << 20),
    )(dequant, resp, slot_map, elist, place.reshape(-1))

    count = n.bit_length() - 1
    sizes = [n >> (k + 1) for k in range(count)]
    return pl.pallas_call(
        functools.partial(reduce_kernel, n, lists),
        out_shape=jax.ShapeDtypeStruct((e_dev, FEAT), jnp.float32),
        in_specs=[pl.BlockSpec(memory_space=pl.ANY)],
        out_specs=whole,
        scratch_shapes=[VMEM((parts, s, tile, 128), jnp.float32) for s in sizes] * 2 + [
            VMEM((parts, n // 2, tile, 128), jnp.float32),
            pltpu.SemaphoreType.DMA((parts, count)),
            pltpu.SemaphoreType.DMA((parts, count)),
            pltpu.SemaphoreType.DMA((parts,)),
        ],
        compiler_params=pltpu.CompilerParams(collective_id=0, has_side_effects=True, vmem_limit_bytes=56 << 20),
    )(table)


def solution(mesh):
    in_specs = (
        P(None, ("parts", "xy"), None, None),
        P(None, ("parts", "xy"), None),
        P(("parts", "xy"), None, None),
        P(("parts", "xy"), None, None),
        P(("parts", "xy"), None),
        P("parts"),
    )
    out_specs = P(("parts", "xy"), None)
    return jax.shard_map(shards, mesh=mesh, in_specs=in_specs, out_specs=out_specs, check_vma=False)
```
